512 devices in a mesh: seq: 64 (over y, x, core), chan: 8 (over z).
Axes of the slice: x: 4, y: 8, z: 8, core: 2. Of those that a mesh axis runs over, the one named last changes fastest.
Arguments:
- out_gate: bfloat16 [16384, 16, 256], P('seq', 'chan'), may hold values from -6 to 6
- in_gate: bfloat16 [16384, 16, 256], P('seq', 'chan'), may hold values from -6 to 6
- values_in: bfloat16 [16384, 16, 256], P('seq', 'chan'), may hold values from -6 to 6
- filter_taps: bfloat16 [16384, 256], P('seq'), may hold values from -1.05 to 1.05
- skip_gain: float32 [16, 256], P('chan'), may hold values from 0.5 to 1.5
- out_cotangent: bfloat16 [16384, 16, 256], P('seq', 'chan'), may hold values from -6 to 6
Outputs:
- mixed: bfloat16 [16384, 16, 256], P('seq', 'chan')
- grad_out_gate: bfloat16 [16384, 16, 256], P('seq', 'chan')
- grad_in_gate: bfloat16 [16384, 16, 256], P('seq', 'chan')
- grad_values: bfloat16 [16384, 16, 256], P('seq', 'chan')
- grad_filter: float32 [16384, 256], P('seq', 'chan')
The draws below stay inside these ranges and needn't reach their ends.
All inputs are finite; a program needn't handle non-finite values.
Results may differ from the reference program's by a relative error of at most 0.0049.
Values may be sent and summed in bfloat16 or wider, within the bound.
No kernel may reach another device: no remote copies, remote signals or barrier semaphores. Data moves between devices by JAX's collectives and lax.ppermute only.
A program may use at most 128 MiB of HBM per device.

```python
import math
import jax
import jax.numpy as jnp
from jax import lax

MEMBERS = 16
GROUPS = 256
TOKENS = 16384


def draw_filter_taps(key, part):
    key = jax.random.fold_in(key, 11)
    rate_key, noise_key = jax.random.split(key)
    seq_total = float(TOKENS)
    shortest = 30.0
    jitter = jnp.clip(jax.random.normal(noise_key, (TOKENS, GROUPS), jnp.float32), -4.0, 4.0)
    fraction = jax.random.uniform(rate_key, (GROUPS,), jnp.float32)
    horizon = shortest * jnp.exp(fraction * jnp.log(4.0 * seq_total / shortest))
    positions = jnp.arange(TOKENS, dtype=jnp.float32)[:, None]
    scaling = jnp.sqrt(jnp.expm1(-2.0 / horizon) / jnp.expm1(-2.0 * seq_total / horizon))
    return (jitter * jnp.exp(-positions / horizon) * scaling).astype(jnp.bfloat16)


def levels(key, extent, cuts, smallest, largest):
    def one(position, parts):
        heights = jax.random.uniform(jax.random.fold_in(jax.random.fold_in(key, 6), position), (parts,), jnp.float32, smallest / len(cuts), largest / len(cuts))
        return jnp.repeat(jnp.exp(heights), extent[position] // parts).reshape((-1,) + (1,) * (len(extent) - position - 1))

    loudness = one(*cuts[0])
    for cut in cuts[1:]:
        loudness = loudness * one(*cut)
    return loudness


def normal_values(own_key, extent, deviation, reach, cuts=(), kind=jnp.bfloat16):
    drawn = jax.random.normal(own_key, extent, jnp.float32) * deviation
    if len(cuts) > 0:
        drawn = levels(own_key, extent, cuts, -0.22, 0.18) * drawn
    return jnp.clip(drawn, min=-reach, max=reach).astype(kind)


def setup_inputs(seed: int = 0) -> dict:
    key_list = jax.random.split(jax.random.key(seed), 7)
    return {
        "out_gate": normal_values(key_list[0], (TOKENS, MEMBERS, GROUPS), 1.0, 6.0, ((0, 64), (1, 8))),
        "in_gate": normal_values(key_list[1], (TOKENS, MEMBERS, GROUPS), 1.0, 6.0, ((0, 64), (1, 8))),
        "values_in": normal_values(key_list[2], (TOKENS, MEMBERS, GROUPS), 1.0, 6.0, ((0, 64), (1, 8))),
        "filter_taps": draw_filter_taps(jax.random.fold_in(key_list[6], 71), 0),
        "skip_gain": jnp.clip(0.5 + 1.0 * jax.random.uniform(key_list[4], (MEMBERS, GROUPS), jnp.float32) ** levels(key_list[4], (MEMBERS, GROUPS), ((0, 8),), -0.2, 0.2), 0.5, 1.5),
        "out_cotangent": normal_values(key_list[5], (TOKENS, MEMBERS, GROUPS), 1.0, 6.0, ((0, 64), (1, 8))),
    }


def reference(out_gate, in_gate, values_in, filter_taps, skip_gain, out_cotangent):
    length = out_gate.shape[0]
    fft_size = 2 * length
    taps_spec = jnp.fft.rfft(filter_taps.astype(jnp.float32), n=fft_size, axis=0)
    mixed_in = (in_gate.astype(jnp.float32) * values_in.astype(jnp.float32)).astype(jnp.bfloat16)
    conv_cot = (out_cotangent.astype(jnp.float32) * out_gate.astype(jnp.float32)).astype(jnp.bfloat16)

    def per_member(pair):
        signal_in, signal_cot = pair
        input_spec = jnp.fft.rfft(signal_in.astype(jnp.float32), n=fft_size, axis=0)
        cot_spec = jnp.fft.rfft(signal_cot.astype(jnp.float32), n=fft_size, axis=0)
        conv_part = jnp.fft.irfft(input_spec * taps_spec, n=fft_size, axis=0)[:length]
        back_part = jnp.fft.irfft(cot_spec * jnp.conj(taps_spec), n=fft_size, axis=0)[:length]
        lag_part = jnp.fft.irfft(cot_spec * jnp.conj(input_spec), n=fft_size, axis=0)[:length]
        return (conv_part, back_part, lag_part)
    conv_all, back_all, lag_all = lax.map(per_member, (jnp.moveaxis(mixed_in, 1, 0), jnp.moveaxis(conv_cot, 1, 0)))
    conv_out = jnp.moveaxis(conv_all, 0, 1)
    back_conv = jnp.moveaxis(back_all, 0, 1)
    mixed_float = mixed_in.astype(jnp.float32)
    cot_float = conv_cot.astype(jnp.float32)
    before_gate = conv_out + skip_gain[None] * mixed_float
    mixed = (out_gate.astype(jnp.float32) * before_gate).astype(jnp.bfloat16)
    grad_out_gate = (out_cotangent.astype(jnp.float32) * before_gate).astype(jnp.bfloat16)
    back_in = back_conv + skip_gain[None] * cot_float
    grad_in_gate = (back_in * values_in.astype(jnp.float32)).astype(jnp.bfloat16)
    grad_values = (back_in * in_gate.astype(jnp.float32)).astype(jnp.bfloat16)
    grad_filter = lax.optimization_barrier(jnp.sum(lag_all, axis=0)) / math.sqrt(length * out_gate.shape[1])
    return (mixed, grad_out_gate, grad_in_gate, grad_values, grad_filter)
```

```python
import math

import jax
import jax.numpy as jnp
import ml_dtypes
import numpy as np
from jax import lax
from jax.experimental import pallas as pl
from jax.experimental.pallas import tpu as pltpu
from jax.sharding import PartitionSpec as P

BLOCKS = 64
ROWS = 256
HALF = ROWS // 2
SIGNALS = 8
GROUPS_HERE = 4
KEPT = 64
FULL = 2 * BLOCKS * ROWS


def split_table(table):
    high = table.astype(ml_dtypes.bfloat16)
    low = (table - high.astype(np.float64)).astype(ml_dtypes.bfloat16)
    return high, low


def tables():
    kept = np.arange(KEPT)[:, None]
    block = np.arange(BLOCKS)[None, :]
    coarse = 2 * math.pi * (((2 * kept + 1) * block) % (4 * BLOCKS)) / (4 * BLOCKS)
    enter_high, enter_low = split_table(np.concatenate([np.cos(coarse), -np.sin(coarse)], axis=0))
    enter = np.concatenate([enter_high, enter_low], axis=1)
    leave_high, leave_low = split_table(
        np.concatenate([np.cos(coarse.T), -np.sin(coarse.T)], axis=1) * (2.0 / FULL)
    )
    leave = np.concatenate([leave_high, leave_high, leave_low], axis=1)
    row = np.arange(ROWS)[None, :]
    twist = 2 * math.pi * (kept + 0.5) * row / FULL
    turn_cos = np.cos(twist).astype(np.float32)
    turn_sin = np.sin(twist).astype(np.float32)
    fine = []
    for odd in (0, 1):
        angle = (
            2
            * math.pi
            * ((np.arange(HALF)[:, None] * (2 * np.arange(HALF)[None, :] + odd)) % ROWS)
            / ROWS
        )
        cos, sin = np.cos(angle), np.sin(angle)
        forth = np.concatenate(
            [np.concatenate([cos, -sin], axis=1), np.concatenate([sin, cos], axis=1)], axis=0
        )
        fine.append((split_table(forth), split_table(forth.T)))
    forth = np.stack([fine[0][0][0], fine[0][0][1], fine[1][0][0], fine[1][0][1]])
    back = np.stack([fine[0][1][0], fine[0][1][1], fine[1][1][0], fine[1][1][1]])
    return enter, leave, turn_cos, turn_sin, forth, back


def mxu(left, right):
    return jnp.dot(left, right, preferred_element_type=jnp.float32)


def halves(value):
    high = value.astype(jnp.bfloat16)
    low = (value - high.astype(jnp.float32)).astype(jnp.bfloat16)
    return high, low


def spectral_kernel(
    recv_ref,
    enter_ref,
    leave_ref,
    cos_ref,
    sin_ref,
    forth_ref,
    back_ref,
    send_ref,
    wide_ref,
    high_ref,
    low_ref,
    spec_ref,
    turn_ref,
):
    signals = 2 * SIGNALS + GROUPS_HERE
    for lane in range(5):
        lanes = slice(lane * HALF, (lane + 1) * HALF)
        wide_ref[lane] = (
            recv_ref[:, :, lanes].astype(jnp.float32).reshape(BLOCKS * SIGNALS, HALF)
        )
    enter = enter_ref[...]
    turn_cos = cos_ref[...]
    turn_sin = sin_ref[...]

    def every(row):
        return pl.ds(row, BLOCKS, stride=SIGNALS)

    for index in range(signals):
        if index < 2 * SIGNALS:
            which, row = divmod(index, SIGNALS)
            places = ((2 * which, row), (2 * which + 1, row))
        else:
            row = index - 2 * SIGNALS
            places = ((4, row), (4, row + GROUPS_HERE))
        taken = jnp.concatenate(
            [wide_ref[lane, every(place), :] for lane, place in places], axis=1
        ).astype(jnp.bfloat16)
        first = mxu(enter, jnp.concatenate([taken, taken], axis=0))
        real, imag = first[:KEPT], first[KEPT:]
        turned_real = real * turn_cos + imag * turn_sin
        turned_imag = imag * turn_cos - real * turn_sin
        for odd in (0, 1):
            sign = 1.0 - 2.0 * odd
            for part, value in enumerate((turned_real, turned_imag)):
                high, low = halves(value[:, :HALF] + sign * value[:, HALF:])
                rows = slice(index * KEPT, (index + 1) * KEPT)
                lanes = slice(part * HALF, (part + 1) * HALF)
                high_ref[odd, rows, lanes] = high
                low_ref[odd, rows, lanes] = low

    def both(matrix_ref, odd, rows):
        high = high_ref[odd, rows, :]
        return (
            mxu(low_ref[odd, rows, :], matrix_ref[2 * odd])
            + mxu(high, matrix_ref[2 * odd + 1])
            + mxu(high, matrix_ref[2 * odd])
        )

    chunk = 4 * KEPT
    for start in range(0, signals * KEPT, chunk):
        for odd in (0, 1):
            spec_ref[odd, start : start + chunk, :] = both(
                forth_ref, odd, slice(start, start + chunk)
            )

    def spectrum(odd, index):
        rows = slice(index * KEPT, (index + 1) * KEPT)
        return spec_ref[odd, rows, :HALF], spec_ref[odd, rows, HALF:]

    def put(odd, index, real, imag):
        rows = slice(index * KEPT, (index + 1) * KEPT)
        for part, value in enumerate((real, imag)):
            high, low = halves(value)
            lanes = slice(part * HALF, (part + 1) * HALF)
            high_ref[odd, rows, lanes] = high
            low_ref[odd, rows, lanes] = low

    for group in range(GROUPS_HERE):
        for odd in (0, 1):
            tap_real, tap_imag = spectrum(odd, 2 * SIGNALS + group)
            lag_real = jnp.zeros((KEPT, HALF), jnp.float32)
            lag_imag = jnp.zeros((KEPT, HALF), jnp.float32)
            for member in range(SIGNALS // GROUPS_HERE):
                index = member * GROUPS_HERE + group
                in_real, in_imag = spectrum(odd, index)
                cot_real, cot_imag = spectrum(odd, SIGNALS + index)
                put(
                    odd,
                    index,
                    in_real * tap_real - in_imag * tap_imag,
                    in_real * tap_imag + in_imag * tap_real,
                )
                put(
                    odd,
                    SIGNALS + index,
                    cot_real * tap_real + cot_imag * tap_imag,
                    cot_imag * tap_real - cot_real * tap_imag,
                )
                lag_real += cot_real * in_real + cot_imag * in_imag
                lag_imag += cot_imag * in_real - cot_real * in_imag
            put(odd, 2 * SIGNALS + group, lag_real, lag_imag)

    for start in range(0, signals * KEPT, chunk):
        rows = slice(start, start + chunk)
        even_part = both(back_ref, 0, rows)
        odd_part = both(back_ref, 1, rows)
        turn_ref[0, rows, :] = even_part + odd_part
        turn_ref[1, rows, :] = even_part - odd_part

    leave = leave_ref[...]
    for index in range(signals):
        rows = slice(index * KEPT, (index + 1) * KEPT)
        real = jnp.concatenate([turn_ref[0, rows, :HALF], turn_ref[1, rows, :HALF]], axis=1)
        imag = jnp.concatenate([turn_ref[0, rows, HALF:], turn_ref[1, rows, HALF:]], axis=1)
        real_high, real_low = halves(real * turn_cos - imag * turn_sin)
        imag_high, imag_low = halves(imag * turn_cos + real * turn_sin)
        result = mxu(
            leave,
            jnp.concatenate(
                [real_high, imag_high, real_low, imag_low, real_high, imag_high], axis=0
            ),
        )
        if index < 2 * SIGNALS:
            which, row = divmod(index, SIGNALS)
            wide_ref[2 * which, every(row), :] = result[:, :HALF]
            wide_ref[2 * which + 1, every(row), :] = result[:, HALF:]
        else:
            row = index - 2 * SIGNALS
            wide_ref[4, every(row), :] = result[:, :HALF]
            wide_ref[4, every(row + GROUPS_HERE), :] = result[:, HALF:]
    for lane in range(5):
        lanes = slice(lane * HALF, (lane + 1) * HALF)
        send_ref[:, :, lanes] = (
            wide_ref[lane].reshape(BLOCKS, SIGNALS, HALF).astype(jnp.bfloat16)
        )


def spectral(received):
    signals = 2 * SIGNALS + GROUPS_HERE
    return pl.pallas_call(
        spectral_kernel,
        out_shape=jax.ShapeDtypeStruct((BLOCKS, SIGNALS, 5 * HALF), jnp.bfloat16),
        in_specs=[pl.BlockSpec(memory_space=pltpu.VMEM)] * 7,
        out_specs=pl.BlockSpec(memory_space=pltpu.VMEM),
        scratch_shapes=[
            pltpu.VMEM((5, BLOCKS * SIGNALS, HALF), jnp.float32),
            pltpu.VMEM((2, signals * KEPT, ROWS), jnp.bfloat16),
            pltpu.VMEM((2, signals * KEPT, ROWS), jnp.bfloat16),
            pltpu.VMEM((2, signals * KEPT, ROWS), jnp.float32),
            pltpu.VMEM((2, signals * KEPT, ROWS), jnp.float32),
        ],
        compiler_params=pltpu.CompilerParams(vmem_limit_bytes=32 * 1024 * 1024),
        cost_estimate=pl.CostEstimate(flops=6_000_000_000, bytes_accessed=3_000_000, transcendentals=0),
        name="spectral",
    )(received, *(jnp.asarray(table) for table in tables()))


def chunks(signal):
    row_count, member_count, group_count = signal.shape
    return (
        signal.reshape(row_count, member_count, BLOCKS, GROUPS_HERE)
        .transpose(2, 1, 3, 0)
        .reshape(BLOCKS, member_count * GROUPS_HERE, row_count)
    )


def unchunks(received, member_count):
    return (
        received.reshape(BLOCKS, member_count, GROUPS_HERE, ROWS)
        .transpose(3, 1, 0, 2)
        .reshape(ROWS, member_count, BLOCKS * GROUPS_HERE)
        .astype(jnp.float32)
    )


def exchange(value, axis):
    return lax.all_to_all(value, axis, split_axis=0, concat_axis=0, tiled=True)


def local(out_gate, in_gate, values_in, filter_taps, skip_gain, out_cotangent):
    row_count, member_count, group_count = out_gate.shape
    chan_count = lax.axis_size("chan")
    mixed_in = (in_gate.astype(jnp.float32) * values_in.astype(jnp.float32)).astype(jnp.bfloat16)
    conv_cot = (out_cotangent.astype(jnp.float32) * out_gate.astype(jnp.float32)).astype(
        jnp.bfloat16
    )
    taps = (
        filter_taps.T.reshape(BLOCKS, GROUPS_HERE, 2, HALF)
        .transpose(0, 2, 1, 3)
        .reshape(BLOCKS, SIGNALS, HALF)
    )
    outgoing = jnp.concatenate([chunks(mixed_in), chunks(conv_cot), taps], axis=2)
    returned = exchange(spectral(exchange(outgoing, "seq")), "seq")
    lag_terms = exchange(
        returned[:, :, 4 * HALF :].reshape(chan_count, -1, SIGNALS, HALF), "chan"
    )
    lag_sum = jnp.sum(lag_terms.astype(jnp.float32), axis=0)
    norm_factor = 1.0 / math.sqrt(BLOCKS * row_count * member_count * chan_count)
    grad_filter = (
        lag_sum.reshape(-1, 2, GROUPS_HERE, HALF).transpose(1, 3, 0, 2).reshape(row_count, -1)
        * norm_factor
    )
    conv_out = unchunks(returned[:, :, : 2 * HALF], member_count)
    back_conv = unchunks(returned[:, :, 2 * HALF : 4 * HALF], member_count)
    before_gate = conv_out + skip_gain[None] * mixed_in.astype(jnp.float32)
    mixed = (out_gate.astype(jnp.float32) * before_gate).astype(jnp.bfloat16)
    grad_out_gate = (out_cotangent.astype(jnp.float32) * before_gate).astype(jnp.bfloat16)
    back_in = back_conv + skip_gain[None] * conv_cot.astype(jnp.float32)
    grad_in_gate = (back_in * values_in.astype(jnp.float32)).astype(jnp.bfloat16)
    grad_values = (back_in * in_gate.astype(jnp.float32)).astype(jnp.bfloat16)
    return (mixed, grad_out_gate, grad_in_gate, grad_values, grad_filter)


def solution(mesh):
    in_specs = (
        P("seq", "chan", None),
        P("seq", "chan", None),
        P("seq", "chan", None),
        P("seq", None),
        P("chan", None),
        P("seq", "chan", None),
    )
    out_specs = (
        P("seq", "chan", None),
        P("seq", "chan", None),
        P("seq", "chan", None),
        P("seq", "chan", None),
        P("seq", "chan"),
    )
    return jax.shard_map(local, mesh=mesh, in_specs=in_specs, out_specs=out_specs, check_vma=False)
```

```python
import math

import jax
import jax.numpy as jnp
import ml_dtypes
import numpy as np
from jax import lax
from jax.experimental import pallas as pl
from jax.experimental.pallas import tpu as pltpu
from jax.sharding import PartitionSpec as P

BLOCKS = 64
ROWS = 256
HALF = ROWS // 2
SIGNALS = 8
GROUPS_HERE = 4
KEPT = 64
FULL = 2 * BLOCKS * ROWS


def split_table(table):
    high = table.astype(ml_dtypes.bfloat16)
    low = (table - high.astype(np.float64)).astype(ml_dtypes.bfloat16)
    return high, low


def tables():
    kept = np.arange(KEPT)[:, None]
    block = np.arange(BLOCKS)[None, :]
    coarse = 2 * math.pi * (((2 * kept + 1) * block) % (4 * BLOCKS)) / (4 * BLOCKS)
    enter_high, enter_low = split_table(np.concatenate([np.cos(coarse), -np.sin(coarse)], axis=0))
    enter = np.concatenate([enter_high, enter_low], axis=1)
    leave_high, leave_low = split_table(
        np.concatenate([np.cos(coarse.T), -np.sin(coarse.T)], axis=1) * (2.0 / FULL)
    )
    leave = np.concatenate(
        [
            np.concatenate([leave_high, leave_high], axis=1),
            np.concatenate([leave_low, np.zeros_like(leave_low)], axis=1),
        ]
    )
    row = np.arange(ROWS)[None, :]
    twist = 2 * math.pi * (kept + 0.5) * row / FULL
    turn_cos = np.cos(twist).astype(np.float32)
    turn_sin = np.sin(twist).astype(np.float32)
    fine = []
    for odd in (0, 1):
        angle = (
            2
            * math.pi
            * ((np.arange(HALF)[:, None] * (2 * np.arange(HALF)[None, :] + odd)) % ROWS)
            / ROWS
        )
        cos, sin = np.cos(angle), np.sin(angle)
        forth = np.concatenate(
            [np.concatenate([cos, -sin], axis=1), np.concatenate([sin, cos], axis=1)], axis=0
        )
        fine.append((split_table(forth), split_table(forth.T)))
    forth, back = (
        np.stack([np.concatenate([high, low, high]) for high, low in (pair[way] for pair in fine)])
        for way in (0, 1)
    )
    return enter, leave, turn_cos, turn_sin, forth, back


def mxu(left, right):
    return jnp.dot(left, right, preferred_element_type=jnp.float32)


def halves(value):
    high = value.astype(jnp.bfloat16)
    low = (value - high.astype(jnp.float32)).astype(jnp.bfloat16)
    return high, low


def spectral_kernel(
    recv_ref,
    enter_ref,
    leave_ref,
    cos_ref,
    sin_ref,
    forth_ref,
    back_ref,
    send_ref,
    wide_ref,
    high_ref,
    low_ref,
    spec_ref,
    turn_ref,
):
    signals = 2 * SIGNALS + GROUPS_HERE
    for lane in range(5):
        lanes = slice(lane * HALF, (lane + 1) * HALF)
        wide_ref[lane] = (
            recv_ref[:, :, lanes].astype(jnp.float32).reshape(BLOCKS * SIGNALS, HALF)
        )
    enter = enter_ref[...]
    turn_cos = cos_ref[...]
    turn_sin = sin_ref[...]

    def every(row):
        return pl.ds(row, BLOCKS, stride=SIGNALS)

    leave = leave_ref[...]
    members = SIGNALS // GROUPS_HERE
    count = 2 * members + 1

    def places(group, item):
        if item == 2 * members:
            return ((4, group), (4, group + GROUPS_HERE))
        which, member = divmod(item, members)
        row = member * GROUPS_HERE + group
        return ((2 * which, row), (2 * which + 1, row))

    def spot(group, item):
        start = (group * count + item) * KEPT
        return slice(start, start + KEPT)

    def put(odd, rows, real, imag):
        for part, value in enumerate((real, imag)):
            high, low = halves(value)
            lanes = slice(part * HALF, (part + 1) * HALF)
            high_ref[odd, rows, lanes] = high
            low_ref[odd, rows, lanes] = low

    def both(matrix_ref, odd, rows):
        high = high_ref[odd, rows, :]
        return mxu(
            jnp.concatenate([low_ref[odd, rows, :], high, high], axis=1), matrix_ref[odd]
        )

    def enter_group(group):
        for item in range(count):
            taken = jnp.concatenate(
                [wide_ref[lane, every(row), :] for lane, row in places(group, item)], axis=1
            ).astype(jnp.bfloat16)
            first = mxu(enter, jnp.concatenate([taken, taken], axis=0))
            real, imag = first[:KEPT], first[KEPT:]
            turned_real = real * turn_cos + imag * turn_sin
            turned_imag = imag * turn_cos - real * turn_sin
            for odd in (0, 1):
                sign = 1.0 - 2.0 * odd
                put(
                    odd,
                    spot(group, item),
                    turned_real[:, :HALF] + sign * turned_real[:, HALF:],
                    turned_imag[:, :HALF] + sign * turned_imag[:, HALF:],
                )

    def forth_group(group):
        rows = slice(group * count * KEPT, (group + 1) * count * KEPT)
        for odd in (0, 1):
            spec_ref[odd, rows, :] = both(forth_ref, odd, rows)

    def multiply_group(group):
        for odd in (0, 1):

            def spectrum(item):
                rows = spot(group, item)
                return spec_ref[odd, rows, :HALF], spec_ref[odd, rows, HALF:]

            tap_real, tap_imag = spectrum(2 * members)
            lag_real = lag_imag = None
            for member in range(members):
                in_real, in_imag = spectrum(member)
                cot_real, cot_imag = spectrum(members + member)
                put(
                    odd,
                    spot(group, member),
                    in_real * tap_real - in_imag * tap_imag,
                    in_real * tap_imag + in_imag * tap_real,
                )
                put(
                    odd,
                    spot(group, members + member),
                    cot_real * tap_real + cot_imag * tap_imag,
                    cot_imag * tap_real - cot_real * tap_imag,
                )
                more_real = cot_real * in_real + cot_imag * in_imag
                more_imag = cot_imag * in_real - cot_real * in_imag
                lag_real = more_real if member == 0 else lag_real + more_real
                lag_imag = more_imag if member == 0 else lag_imag + more_imag
            put(odd, spot(group, 2 * members), lag_real, lag_imag)

    def back_group(group):
        rows = slice(group * count * KEPT, (group + 1) * count * KEPT)
        even_part = both(back_ref, 0, rows)
        odd_part = both(back_ref, 1, rows)
        turn_ref[0, rows, :] = even_part + odd_part
        turn_ref[1, rows, :] = even_part - odd_part

    def leave_group(group):
        for item in range(count):
            rows = spot(group, item)
            real = jnp.concatenate([turn_ref[0, rows, :HALF], turn_ref[1, rows, :HALF]], axis=1)
            imag = jnp.concatenate([turn_ref[0, rows, HALF:], turn_ref[1, rows, HALF:]], axis=1)
            real_high, real_low = halves(real * turn_cos - imag * turn_sin)
            imag_high, imag_low = halves(imag * turn_cos + real * turn_sin)
            result = mxu(
                leave,
                jnp.concatenate([real_high, imag_high, real_low, imag_low], axis=0),
            )
            result = result[:BLOCKS] + result[BLOCKS:]
            for part, (lane, row) in enumerate(places(group, item)):
                wide_ref[lane, every(row), :] = result[:, part * HALF : (part + 1) * HALF]

    for step in range(GROUPS_HERE + 4):
        for lag, stage in enumerate(
            (enter_group, forth_group, multiply_group, back_group, leave_group)
        ):
            if 0 <= step - lag < GROUPS_HERE:
                stage(step - lag)
    for lane in range(5):
        lanes = slice(lane * HALF, (lane + 1) * HALF)
        send_ref[:, :, lanes] = (
            wide_ref[lane].reshape(BLOCKS, SIGNALS, HALF).astype(jnp.bfloat16)
        )


def spectral(received):
    signals = 2 * SIGNALS + GROUPS_HERE
    return pl.pallas_call(
        spectral_kernel,
        out_shape=jax.ShapeDtypeStruct((BLOCKS, SIGNALS, 5 * HALF), jnp.bfloat16),
        in_specs=[pl.BlockSpec(memory_space=pltpu.VMEM)] * 7,
        out_specs=pl.BlockSpec(memory_space=pltpu.VMEM),
        scratch_shapes=[
            pltpu.VMEM((5, BLOCKS * SIGNALS, HALF), jnp.float32),
            pltpu.VMEM((2, signals * KEPT, ROWS), jnp.bfloat16),
            pltpu.VMEM((2, signals * KEPT, ROWS), jnp.bfloat16),
            pltpu.VMEM((2, signals * KEPT, ROWS), jnp.float32),
            pltpu.VMEM((2, signals * KEPT, ROWS), jnp.float32),
        ],
        compiler_params=pltpu.CompilerParams(vmem_limit_bytes=32 * 1024 * 1024),
        cost_estimate=pl.CostEstimate(flops=6_000_000_000, bytes_accessed=3_000_000, transcendentals=0),
        name="spectral",
    )(received, *(jnp.asarray(table) for table in tables()))


def gate_kernel(
    out_gate_ref,
    in_gate_ref,
    values_ref,
    taps_ref,
    cot_ref,
    send_ref,
    gates_ref,
    held_taps_ref,
    arrived,
):
    sources = (in_gate_ref, values_ref, cot_ref, out_gate_ref)
    copies = [
        pltpu.make_async_copy(source, gates_ref.at[slot], arrived.at[slot])
        for slot, source in enumerate(sources)
    ]
    copies.append(pltpu.make_async_copy(taps_ref, held_taps_ref, arrived.at[len(sources)]))
    for copy in copies:
        copy.start()

    row = lax.broadcasted_iota(jnp.int32, (2 * ROWS, 2 * ROWS), 0)
    column = lax.broadcasted_iota(jnp.int32, (2 * ROWS, 2 * ROWS), 1)
    parted = (row == column % ROWS * 2 + column // ROWS).astype(jnp.float32)
    parted = parted.astype(jnp.bfloat16)
    plain = (row == column)[:ROWS, :ROWS].astype(jnp.float32).astype(jnp.bfloat16)

    def turned(value, order):
        return lax.dot_general(
            value, order, (((0,), (0,)), ((), ())), preferred_element_type=jnp.float32
        ).astype(jnp.bfloat16)

    def send(part, lanes, value):
        rows = slice(part * GROUPS_HERE, (part + 1) * GROUPS_HERE)
        send_ref[:, rows, lanes] = value.reshape(BLOCKS, GROUPS_HERE, -1)

    for which in range(2):
        left, right = 2 * which, 2 * which + 1
        copies[left].wait()
        copies[right].wait()
        product = gates_ref[left].reshape(2 * ROWS, ROWS).astype(jnp.float32) * gates_ref[
            right
        ].reshape(2 * ROWS, ROWS).astype(jnp.float32)
        signal = turned(product.astype(jnp.bfloat16), parted)
        for member in range(2):
            send(
                member,
                slice(which * ROWS, (which + 1) * ROWS),
                signal[:, member * ROWS : (member + 1) * ROWS],
            )
    copies[-1].wait()
    taps = turned(held_taps_ref[...], plain)
    for half in range(2):
        send(half, slice(2 * ROWS, None), taps[:, half * HALF : (half + 1) * HALF])


def gated_chunks(out_gate, in_gate, values_in, filter_taps, out_cotangent):
    return pl.pallas_call(
        gate_kernel,
        out_shape=jax.ShapeDtypeStruct((BLOCKS, SIGNALS, 5 * HALF), jnp.bfloat16),
        in_specs=[pl.BlockSpec(memory_space=pl.ANY)] * 5,
        out_specs=pl.BlockSpec(memory_space=pltpu.VMEM),
        scratch_shapes=[
            pltpu.VMEM((4, ROWS, 2, ROWS), jnp.bfloat16),
            pltpu.VMEM((ROWS, ROWS), jnp.bfloat16),
            pltpu.SemaphoreType.DMA((5,)),
        ],
        cost_estimate=pl.CostEstimate(
            flops=400_000_000, bytes_accessed=2_000_000, transcendentals=0
        ),
        name="gates",
    )(out_gate, in_gate, values_in, filter_taps, out_cotangent)


def unchunks(received, member_count):
    return (
        received.reshape(BLOCKS, member_count, GROUPS_HERE, ROWS)
        .transpose(3, 1, 0, 2)
        .reshape(ROWS, member_count, BLOCKS * GROUPS_HERE)
        .astype(jnp.float32)
    )


def exchange(value, axis):
    return lax.all_to_all(value, axis, split_axis=0, concat_axis=0, tiled=True)


def local(out_gate, in_gate, values_in, filter_taps, skip_gain, out_cotangent):
    row_count, member_count, group_count = out_gate.shape
    chan_count = lax.axis_size("chan")
    outgoing = gated_chunks(out_gate, in_gate, values_in, filter_taps, out_cotangent)
    returned = exchange(spectral(exchange(outgoing, "seq")), "seq")
    lag_terms = exchange(
        returned[:, :, 4 * HALF :].reshape(chan_count, -1, SIGNALS, HALF), "chan"
    )
    norm_factor = 1.0 / math.sqrt(BLOCKS * row_count * member_count * chan_count)
    lag_sum = jnp.sum(lag_terms.astype(jnp.float32), axis=0)
    grad_filter = (
        lag_sum.reshape(-1, 2, GROUPS_HERE, HALF).transpose(1, 3, 0, 2).reshape(row_count, -1)
        * norm_factor
    )
    mixed_in = (in_gate.astype(jnp.float32) * values_in.astype(jnp.float32)).astype(jnp.bfloat16)
    conv_cot = (out_cotangent.astype(jnp.float32) * out_gate.astype(jnp.float32)).astype(
        jnp.bfloat16
    )
    conv_out = unchunks(returned[:, :, : 2 * HALF], member_count)
    back_conv = unchunks(returned[:, :, 2 * HALF : 4 * HALF], member_count)
    before_gate = conv_out + skip_gain[None] * mixed_in.astype(jnp.float32)
    mixed = (out_gate.astype(jnp.float32) * before_gate).astype(jnp.bfloat16)
    grad_out_gate = (out_cotangent.astype(jnp.float32) * before_gate).astype(jnp.bfloat16)
    back_in = back_conv + skip_gain[None] * conv_cot.astype(jnp.float32)
    grad_in_gate = (back_in * values_in.astype(jnp.float32)).astype(jnp.bfloat16)
    grad_values = (back_in * in_gate.astype(jnp.float32)).astype(jnp.bfloat16)
    return (mixed, grad_out_gate, grad_in_gate, grad_values, grad_filter)


def solution(mesh):
    in_specs = (
        P("seq", "chan", None),
        P("seq", "chan", None),
        P("seq", "chan", None),
        P("seq", None),
        P("chan", None),
        P("seq", "chan", None),
    )
    out_specs = (
        P("seq", "chan", None),
        P("seq", "chan", None),
        P("seq", "chan", None),
        P("seq", "chan", None),
        P("seq", "chan"),
    )
    return jax.shard_map(local, mesh=mesh, in_specs=in_specs, out_specs=out_specs, check_vma=False)
```

```python
import math

import jax
import jax.numpy as jnp
import ml_dtypes
import numpy as np
from jax import lax
from jax.experimental import pallas as pl
from jax.experimental.pallas import tpu as pltpu
from jax.sharding import PartitionSpec as P

BLOCKS = 64
ROWS = 256
HALF = ROWS // 2
SIGNALS = 8
GROUPS_HERE = 4
KEPT = 64
FULL = 2 * BLOCKS * ROWS


def split_table(table):
    high = table.astype(ml_dtypes.bfloat16)
    low = (table - high.astype(np.float64)).astype(ml_dtypes.bfloat16)
    return high, low


def tables():
    kept = np.arange(KEPT)[:, None]
    block = np.arange(BLOCKS)[None, :]
    coarse = 2 * math.pi * (((2 * kept + 1) * block) % (4 * BLOCKS)) / (4 * BLOCKS)
    enter_high, enter_low = split_table(np.concatenate([np.cos(coarse), -np.sin(coarse)], axis=0))
    enter = np.concatenate([enter_high, enter_low], axis=1)
    leave_high, leave_low = split_table(
        np.concatenate([np.cos(coarse.T), -np.sin(coarse.T)], axis=1) * (2.0 / FULL)
    )
    leave = np.concatenate(
        [
            np.concatenate([leave_high, leave_high], axis=1),
            np.concatenate([leave_low, np.zeros_like(leave_low)], axis=1),
        ]
    )
    row = np.arange(ROWS)[None, :]
    twist = 2 * math.pi * (kept + 0.5) * row / FULL
    turn_cos = np.cos(twist).astype(np.float32)
    turn_sin = np.sin(twist).astype(np.float32)
    fine = []
    for odd in (0, 1):
        angle = (
            2
            * math.pi
            * ((np.arange(HALF)[:, None] * (2 * np.arange(HALF)[None, :] + odd)) % ROWS)
            / ROWS
        )
        cos, sin = np.cos(angle), np.sin(angle)
        forth = np.concatenate(
            [np.concatenate([cos, -sin], axis=1), np.concatenate([sin, cos], axis=1)], axis=0
        )
        fine.append((split_table(forth), split_table(forth.T)))
    forth, back = (
        np.stack([np.concatenate([high, low, high]) for high, low in (pair[way] for pair in fine)])
        for way in (0, 1)
    )
    return enter, leave, turn_cos, turn_sin, forth, back


def mxu(left, right):
    return jnp.dot(left, right, preferred_element_type=jnp.float32)


def halves(value):
    high = value.astype(jnp.bfloat16)
    low = (value - high.astype(jnp.float32)).astype(jnp.bfloat16)
    return high, low


def spectral_kernel(
    recv_ref,
    enter_ref,
    leave_ref,
    cos_ref,
    sin_ref,
    forth_ref,
    back_ref,
    send_ref,
    wide_ref,
    high_ref,
    low_ref,
    spec_ref,
    turn_ref,
):
    signals = 2 * SIGNALS + GROUPS_HERE
    for lane in range(5):
        lanes = slice(lane * HALF, (lane + 1) * HALF)
        wide_ref[lane] = (
            recv_ref[:, :, lanes].astype(jnp.float32).reshape(BLOCKS * SIGNALS, HALF)
        )
    enter = enter_ref[...]
    turn_cos = cos_ref[...]
    turn_sin = sin_ref[...]

    def every(row):
        return pl.ds(row, BLOCKS, stride=SIGNALS)

    leave = leave_ref[...]
    members = SIGNALS // GROUPS_HERE
    count = 2 * members + 1

    def places(group, item):
        if item == 2 * members:
            return ((4, group), (4, group + GROUPS_HERE))
        which, member = divmod(item, members)
        row = member * GROUPS_HERE + group
        return ((2 * which, row), (2 * which + 1, row))

    def spot(group, item):
        start = (group * count + item) * KEPT
        return slice(start, start + KEPT)

    def put(odd, rows, real, imag):
        for part, value in enumerate((real, imag)):
            high, low = halves(value)
            lanes = slice(part * HALF, (part + 1) * HALF)
            high_ref[odd, rows, lanes] = high
            low_ref[odd, rows, lanes] = low

    def both(matrix_ref, odd, rows):
        high = high_ref[odd, rows, :]
        return mxu(
            jnp.concatenate([low_ref[odd, rows, :], high, high], axis=1), matrix_ref[odd]
        )

    def enter_group(group):
        for item in range(count):
            taken = jnp.concatenate(
                [wide_ref[lane, every(row), :] for lane, row in places(group, item)], axis=1
            ).astype(jnp.bfloat16)
            first = mxu(enter, jnp.concatenate([taken, taken], axis=0))
            real, imag = first[:KEPT], first[KEPT:]
            turned_real = real * turn_cos + imag * turn_sin
            turned_imag = imag * turn_cos - real * turn_sin
            for odd in (0, 1):
                sign = 1.0 - 2.0 * odd
                put(
                    odd,
                    spot(group, item),
                    turned_real[:, :HALF] + sign * turned_real[:, HALF:],
                    turned_imag[:, :HALF] + sign * turned_imag[:, HALF:],
                )

    def forth_group(group):
        rows = slice(group * count * KEPT, (group + 1) * count * KEPT)
        for odd in (0, 1):
            spec_ref[odd, rows, :] = both(forth_ref, odd, rows)

    def multiply_group(group):
        for odd in (0, 1):

            def spectrum(item):
                rows = spot(group, item)
                return spec_ref[odd, rows, :HALF], spec_ref[odd, rows, HALF:]

            tap_real, tap_imag = spectrum(2 * members)
            lag_real = lag_imag = None
            for member in range(members):
                in_real, in_imag = spectrum(member)
                cot_real, cot_imag = spectrum(members + member)
                put(
                    odd,
                    spot(group, member),
                    in_real * tap_real - in_imag * tap_imag,
                    in_real * tap_imag + in_imag * tap_real,
                )
                put(
                    odd,
                    spot(group, members + member),
                    cot_real * tap_real + cot_imag * tap_imag,
                    cot_imag * tap_real - cot_real * tap_imag,
                )
                more_real = cot_real * in_real + cot_imag * in_imag
                more_imag = cot_imag * in_real - cot_real * in_imag
                lag_real = more_real if member == 0 else lag_real + more_real
                lag_imag = more_imag if member == 0 else lag_imag + more_imag
            put(odd, spot(group, 2 * members), lag_real, lag_imag)

    def back_group(group):
        rows = slice(group * count * KEPT, (group + 1) * count * KEPT)
        even_part = both(back_ref, 0, rows)
        odd_part = both(back_ref, 1, rows)
        turn_ref[0, rows, :] = even_part + odd_part
        turn_ref[1, rows, :] = even_part - odd_part

    def leave_group(group):
        for item in range(count):
            rows = spot(group, item)
            real = jnp.concatenate([turn_ref[0, rows, :HALF], turn_ref[1, rows, :HALF]], axis=1)
            imag = jnp.concatenate([turn_ref[0, rows, HALF:], turn_ref[1, rows, HALF:]], axis=1)
            real_high, real_low = halves(real * turn_cos - imag * turn_sin)
            imag_high, imag_low = halves(imag * turn_cos + real * turn_sin)
            result = mxu(
                leave,
                jnp.concatenate([real_high, imag_high, real_low, imag_low], axis=0),
            )
            result = result[:BLOCKS] + result[BLOCKS:]
            for part, (lane, row) in enumerate(places(group, item)):
                wide_ref[lane, every(row), :] = result[:, part * HALF : (part + 1) * HALF]

    for step in range(GROUPS_HERE + 4):
        for lag, stage in enumerate(
            (enter_group, forth_group, multiply_group, back_group, leave_group)
        ):
            if 0 <= step - lag < GROUPS_HERE:
                stage(step - lag)
    for lane in range(5):
        lanes = slice(lane * HALF, (lane + 1) * HALF)
        send_ref[:, :, lanes] = (
            wide_ref[lane].reshape(BLOCKS, SIGNALS, HALF).astype(jnp.bfloat16)
        )


def spectral(received):
    signals = 2 * SIGNALS + GROUPS_HERE
    return pl.pallas_call(
        spectral_kernel,
        out_shape=jax.ShapeDtypeStruct((BLOCKS, SIGNALS, 5 * HALF), jnp.bfloat16),
        in_specs=[pl.BlockSpec(memory_space=pltpu.VMEM)] * 7,
        out_specs=pl.BlockSpec(memory_space=pltpu.VMEM),
        scratch_shapes=[
            pltpu.VMEM((5, BLOCKS * SIGNALS, HALF), jnp.float32),
            pltpu.VMEM((2, signals * KEPT, ROWS), jnp.bfloat16),
            pltpu.VMEM((2, signals * KEPT, ROWS), jnp.bfloat16),
            pltpu.VMEM((2, signals * KEPT, ROWS), jnp.float32),
            pltpu.VMEM((2, signals * KEPT, ROWS), jnp.float32),
        ],
        compiler_params=pltpu.CompilerParams(vmem_limit_bytes=32 * 1024 * 1024),
        cost_estimate=pl.CostEstimate(flops=6_000_000_000, bytes_accessed=3_000_000, transcendentals=0),
        name="spectral",
    )(received, *(jnp.asarray(table) for table in tables()))


def gate_kernel(
    out_gate_ref,
    in_gate_ref,
    values_ref,
    taps_ref,
    cot_ref,
    send_ref,
    gates_ref,
    held_taps_ref,
    arrived,
):
    sources = (in_gate_ref, values_ref, cot_ref, out_gate_ref)
    copies = [
        pltpu.make_async_copy(source, gates_ref.at[slot], arrived.at[slot])
        for slot, source in enumerate(sources)
    ]
    copies.append(pltpu.make_async_copy(taps_ref, held_taps_ref, arrived.at[len(sources)]))
    for copy in copies:
        copy.start()

    row = lax.broadcasted_iota(jnp.int32, (2 * ROWS, 2 * ROWS), 0)
    column = lax.broadcasted_iota(jnp.int32, (2 * ROWS, 2 * ROWS), 1)
    parted = (row == column % ROWS * 2 + column // ROWS).astype(jnp.float32)
    parted = parted.astype(jnp.bfloat16)
    plain = (row == column)[:ROWS, :ROWS].astype(jnp.float32).astype(jnp.bfloat16)

    def turned(value, order):
        return lax.dot_general(
            value, order, (((0,), (0,)), ((), ())), preferred_element_type=jnp.float32
        ).astype(jnp.bfloat16)

    def send(part, lanes, value):
        rows = slice(part * GROUPS_HERE, (part + 1) * GROUPS_HERE)
        send_ref[:, rows, lanes] = value.reshape(BLOCKS, GROUPS_HERE, -1)

    for which in range(2):
        left, right = 2 * which, 2 * which + 1
        copies[left].wait()
        copies[right].wait()
        product = gates_ref[left].reshape(2 * ROWS, ROWS).astype(jnp.float32) * gates_ref[
            right
        ].reshape(2 * ROWS, ROWS).astype(jnp.float32)
        signal = turned(product.astype(jnp.bfloat16), parted)
        for member in range(2):
            send(
                member,
                slice(which * ROWS, (which + 1) * ROWS),
                signal[:, member * ROWS : (member + 1) * ROWS],
            )
    copies[-1].wait()
    taps = turned(held_taps_ref[...], plain)
    for half in range(2):
        send(half, slice(2 * ROWS, None), taps[:, half * HALF : (half + 1) * HALF])


def gated_chunks(out_gate, in_gate, values_in, filter_taps, out_cotangent):
    return pl.pallas_call(
        gate_kernel,
        out_shape=jax.ShapeDtypeStruct((BLOCKS, SIGNALS, 5 * HALF), jnp.bfloat16),
        in_specs=[pl.BlockSpec(memory_space=pltpu.HBM)] * 5,
        out_specs=pl.BlockSpec(memory_space=pltpu.VMEM),
        scratch_shapes=[
            pltpu.VMEM((4, ROWS, 2, ROWS), jnp.bfloat16),
            pltpu.VMEM((ROWS, ROWS), jnp.bfloat16),
            pltpu.SemaphoreType.DMA((5,)),
        ],
        compiler_params=pltpu.CompilerParams(vmem_limit_bytes=16 * 1024 * 1024),
        cost_estimate=pl.CostEstimate(
            flops=400_000_000, bytes_accessed=2_000_000, transcendentals=0
        ),
        name="gates",
    )(
        *(
            pltpu.with_memory_space_constraint(value, pltpu.HBM)
            for value in (out_gate, in_gate, values_in, filter_taps, out_cotangent)
        )
    )


def unchunks(received, member_count):
    return (
        received.reshape(BLOCKS, member_count, GROUPS_HERE, ROWS)
        .transpose(3, 1, 0, 2)
        .reshape(ROWS, member_count, BLOCKS * GROUPS_HERE)
        .astype(jnp.float32)
    )


def rounded(value):
    return lax.reduce_precision(value, exponent_bits=8, mantissa_bits=7)


def exchange(value, axis):
    return lax.all_to_all(value, axis, split_axis=0, concat_axis=0, tiled=True)


def local(out_gate, in_gate, values_in, filter_taps, skip_gain, out_cotangent):
    row_count, member_count, group_count = out_gate.shape
    chan_count = lax.axis_size("chan")
    outgoing = gated_chunks(out_gate, in_gate, values_in, filter_taps, out_cotangent)
    returned = exchange(spectral(exchange(outgoing, "seq")), "seq")
    lag_terms = exchange(
        returned[:, :, 4 * HALF :].reshape(chan_count, -1, SIGNALS, HALF), "chan"
    )
    norm_factor = 1.0 / math.sqrt(BLOCKS * row_count * member_count * chan_count)
    lag_sum = jnp.sum(lag_terms.astype(jnp.float32), axis=0)
    grad_filter = (
        lag_sum.reshape(-1, 2, GROUPS_HERE, HALF).transpose(1, 3, 0, 2).reshape(row_count, -1)
        * norm_factor
    )
    mixed_in = rounded(in_gate.astype(jnp.float32) * values_in.astype(jnp.float32))
    conv_cot = rounded(out_cotangent.astype(jnp.float32) * out_gate.astype(jnp.float32))
    conv_out = unchunks(returned[:, :, : 2 * HALF], member_count)
    back_conv = unchunks(returned[:, :, 2 * HALF : 4 * HALF], member_count)
    before_gate = conv_out + skip_gain[None] * mixed_in
    mixed = (out_gate.astype(jnp.float32) * before_gate).astype(jnp.bfloat16)
    grad_out_gate = (out_cotangent.astype(jnp.float32) * before_gate).astype(jnp.bfloat16)
    back_in = back_conv + skip_gain[None] * conv_cot
    grad_in_gate = (back_in * values_in.astype(jnp.float32)).astype(jnp.bfloat16)
    grad_values = (back_in * in_gate.astype(jnp.float32)).astype(jnp.bfloat16)
    return (mixed, grad_out_gate, grad_in_gate, grad_values, grad_filter)


def solution(mesh):
    in_specs = (
        P("seq", "chan", None),
        P("seq", "chan", None),
        P("seq", "chan", None),
        P("seq", None),
        P("chan", None),
        P("seq", "chan", None),
    )
    out_specs = (
        P("seq", "chan", None),
        P("seq", "chan", None),
        P("seq", "chan", None),
        P("seq", "chan", None),
        P("seq", "chan"),
    )
    return jax.shard_map(local, mesh=mesh, in_specs=in_specs, out_specs=out_specs, check_vma=False)
```

```python
import math

import jax
import jax.numpy as jnp
import ml_dtypes
import numpy as np
from jax import lax
from jax.experimental import pallas as pl
from jax.experimental.pallas import tpu as pltpu
from jax.sharding import PartitionSpec as P

BLOCKS = 64
ROWS = 256
HALF = ROWS // 2
SIGNALS = 8
GROUPS_HERE = 4
KEPT = 64
TILE = 16
FULL = 2 * BLOCKS * ROWS


def split_table(table):
    high = table.astype(ml_dtypes.bfloat16)
    low = (table - high.astype(np.float64)).astype(ml_dtypes.bfloat16)
    return high, low


def tables():
    kept = np.arange(KEPT)[:, None]
    block = np.arange(BLOCKS)[None, :]
    coarse = 2 * math.pi * (((2 * kept + 1) * block) % (4 * BLOCKS)) / (4 * BLOCKS)
    paired = np.stack([np.cos(coarse), -np.sin(coarse)]).reshape(2, -1, TILE, BLOCKS)
    enter_high, enter_low = split_table(paired.swapaxes(0, 1).reshape(2 * KEPT, BLOCKS))
    enter = np.concatenate([enter_high, enter_low], axis=1)
    leave_high, leave_low = split_table(
        np.concatenate([np.cos(coarse.T), -np.sin(coarse.T)], axis=1) * (2.0 / FULL)
    )
    leave = np.concatenate(
        [
            np.concatenate([leave_high, leave_high], axis=1),
            np.concatenate([leave_low, np.zeros_like(leave_low)], axis=1),
        ]
    )
    row = np.arange(ROWS)[None, :]
    twist = 2 * math.pi * (kept + 0.5) * row / FULL
    turn_cos = np.cos(twist).astype(np.float32)
    turn_sin = np.sin(twist).astype(np.float32)
    fine = []
    for odd in (0, 1):
        angle = (
            2
            * math.pi
            * ((np.arange(HALF)[:, None] * (2 * np.arange(HALF)[None, :] + odd)) % ROWS)
            / ROWS
        )
        cos, sin = np.cos(angle), np.sin(angle)
        forth = np.concatenate(
            [np.concatenate([cos, -sin], axis=1), np.concatenate([sin, cos], axis=1)], axis=0
        )
        fine.append((split_table(forth), split_table(forth.T)))
    forth, back = (
        np.stack([np.concatenate([high, low, high]) for high, low in (pair[way] for pair in fine)])
        for way in (0, 1)
    )
    return enter, leave, turn_cos, turn_sin, forth, back


def mxu(left, right):
    return jnp.dot(left, right, preferred_element_type=jnp.float32)


def halves(value):
    high = value.astype(jnp.bfloat16)
    low = (value - high.astype(jnp.float32)).astype(jnp.bfloat16)
    return high, low


def spectral_kernel(
    recv_ref,
    enter_ref,
    leave_ref,
    cos_ref,
    sin_ref,
    forth_ref,
    back_ref,
    send_ref,
    wide_ref,
    high_ref,
    low_ref,
    spec_ref,
    turn_ref,
):
    signals = 2 * SIGNALS + GROUPS_HERE
    for lane in range(5):
        lanes = slice(lane * HALF, (lane + 1) * HALF)
        wide_ref[lane] = (
            recv_ref[:, :, lanes].astype(jnp.float32).reshape(BLOCKS * SIGNALS, HALF)
        )
    enter = enter_ref[...]

    def every(row):
        return pl.ds(row, BLOCKS, stride=SIGNALS)

    leave = leave_ref[...]
    members = SIGNALS // GROUPS_HERE
    count = 2 * members + 1

    def places(group, item):
        if item == 2 * members:
            return ((4, group), (4, group + GROUPS_HERE))
        which, member = divmod(item, members)
        row = member * GROUPS_HERE + group
        return ((2 * which, row), (2 * which + 1, row))

    def spot(group, item):
        start = (group * count + item) * KEPT
        return slice(start, start + KEPT)

    def put(odd, rows, real, imag):
        for part, value in enumerate((real, imag)):
            high, low = halves(value)
            lanes = slice(part * HALF, (part + 1) * HALF)
            high_ref[odd, rows, lanes] = high
            low_ref[odd, rows, lanes] = low

    def both(matrix_ref, odd, rows):
        high = high_ref[odd, rows, :]
        return mxu(
            jnp.concatenate([low_ref[odd, rows, :], high, high], axis=1), matrix_ref[odd]
        )

    def enter_group(group):
        for item in range(count):
            taken = jnp.concatenate(
                [wide_ref[lane, every(row), :] for lane, row in places(group, item)], axis=1
            ).astype(jnp.bfloat16)
            first = mxu(enter, jnp.concatenate([taken, taken], axis=0))
            start = spot(group, item).start
            for tile in range(0, KEPT, TILE):
                real = first[2 * tile : 2 * tile + TILE]
                imag = first[2 * tile + TILE : 2 * tile + 2 * TILE]
                turn_cos = cos_ref[tile : tile + TILE, :]
                turn_sin = sin_ref[tile : tile + TILE, :]
                turned_real = real * turn_cos + imag * turn_sin
                turned_imag = imag * turn_cos - real * turn_sin
                rows = slice(start + tile, start + tile + TILE)
                near_real, far_real = turned_real[:, :HALF], turned_real[:, HALF:]
                near_imag, far_imag = turned_imag[:, :HALF], turned_imag[:, HALF:]
                put(0, rows, near_real + far_real, near_imag + far_imag)
                put(1, rows, near_real - far_real, near_imag - far_imag)

    def forth_group(group):
        rows = slice(group * count * KEPT, (group + 1) * count * KEPT)
        for odd in (0, 1):
            spec_ref[odd, rows, :] = both(forth_ref, odd, rows)

    def multiply_group(group):
        for odd in (0, 1):
            for tile in range(0, KEPT, TILE):

                def tiled(item):
                    start = spot(group, item).start + tile
                    return slice(start, start + TILE)

                def spectrum(item):
                    rows = tiled(item)
                    return spec_ref[odd, rows, :HALF], spec_ref[odd, rows, HALF:]

                tap_real, tap_imag = spectrum(2 * members)
                lag_real = lag_imag = None
                for member in range(members):
                    in_real, in_imag = spectrum(member)
                    cot_real, cot_imag = spectrum(members + member)
                    put(
                        odd,
                        tiled(member),
                        in_real * tap_real - in_imag * tap_imag,
                        in_real * tap_imag + in_imag * tap_real,
                    )
                    put(
                        odd,
                        tiled(members + member),
                        cot_real * tap_real + cot_imag * tap_imag,
                        cot_imag * tap_real - cot_real * tap_imag,
                    )
                    more_real = cot_real * in_real + cot_imag * in_imag
                    more_imag = cot_imag * in_real - cot_real * in_imag
                    lag_real = more_real if member == 0 else lag_real + more_real
                    lag_imag = more_imag if member == 0 else lag_imag + more_imag
                put(odd, tiled(2 * members), lag_real, lag_imag)

    def back_group(group):
        rows = slice(group * count * KEPT, (group + 1) * count * KEPT)
        for odd in (0, 1):
            turn_ref[odd, rows, :] = both(back_ref, odd, rows)

    def leave_group(group):
        for item in range(count):
            start = spot(group, item).start
            pieces = [[], [], [], []]
            for tile in range(0, KEPT, TILE):
                rows = slice(start + tile, start + tile + TILE)
                turn_cos = cos_ref[tile : tile + TILE, :]
                turn_sin = sin_ref[tile : tile + TILE, :]
                even, odd = turn_ref[0, rows, :], turn_ref[1, rows, :]
                near, far = even + odd, even - odd
                real = jnp.concatenate([near[:, :HALF], far[:, :HALF]], axis=1)
                imag = jnp.concatenate([near[:, HALF:], far[:, HALF:]], axis=1)
                real_high, real_low = halves(real * turn_cos - imag * turn_sin)
                imag_high, imag_low = halves(imag * turn_cos + real * turn_sin)
                for kept, piece in zip(pieces, (real_high, imag_high, real_low, imag_low)):
                    kept.append(piece)
            result = mxu(leave, jnp.concatenate(sum(pieces, []), axis=0))
            result = result[:BLOCKS] + result[BLOCKS:]
            for part, (lane, row) in enumerate(places(group, item)):
                wide_ref[lane, every(row), :] = result[:, part * HALF : (part + 1) * HALF]

    for step in range(GROUPS_HERE + 4):
        for lag, stage in enumerate(
            (enter_group, forth_group, multiply_group, back_group, leave_group)
        ):
            if 0 <= step - lag < GROUPS_HERE:
                stage(step - lag)
    for lane in range(5):
        lanes = slice(lane * HALF, (lane + 1) * HALF)
        send_ref[:, :, lanes] = (
            wide_ref[lane].reshape(BLOCKS, SIGNALS, HALF).astype(jnp.bfloat16)
        )


def spectral(received):
    signals = 2 * SIGNALS + GROUPS_HERE
    return pl.pallas_call(
        spectral_kernel,
        out_shape=jax.ShapeDtypeStruct((BLOCKS, SIGNALS, 5 * HALF), jnp.bfloat16),
        in_specs=[pl.BlockSpec(memory_space=pltpu.VMEM)] * 7,
        out_specs=pl.BlockSpec(memory_space=pltpu.VMEM),
        scratch_shapes=[
            pltpu.VMEM((5, BLOCKS * SIGNALS, HALF), jnp.float32),
            pltpu.VMEM((2, signals * KEPT, ROWS), jnp.bfloat16),
            pltpu.VMEM((2, signals * KEPT, ROWS), jnp.bfloat16),
            pltpu.VMEM((2, signals * KEPT, ROWS), jnp.float32),
            pltpu.VMEM((2, signals * KEPT, ROWS), jnp.float32),
        ],
        compiler_params=pltpu.CompilerParams(vmem_limit_bytes=32 * 1024 * 1024),
        cost_estimate=pl.CostEstimate(flops=6_000_000_000, bytes_accessed=3_000_000, transcendentals=0),
        name="spectral",
    )(received, *(jnp.asarray(table) for table in tables()))


def gate_kernel(
    out_gate_ref,
    in_gate_ref,
    values_ref,
    taps_ref,
    cot_ref,
    send_ref,
    gates_ref,
    held_taps_ref,
    arrived,
):
    sources = (in_gate_ref, values_ref, cot_ref, out_gate_ref)
    copies = [
        pltpu.make_async_copy(source, gates_ref.at[slot], arrived.at[slot])
        for slot, source in enumerate(sources)
    ]
    copies.append(pltpu.make_async_copy(taps_ref, held_taps_ref, arrived.at[len(sources)]))
    for copy in copies:
        copy.start()

    row = lax.broadcasted_iota(jnp.int32, (2 * ROWS, 2 * ROWS), 0)
    column = lax.broadcasted_iota(jnp.int32, (2 * ROWS, 2 * ROWS), 1)
    parted = (row == column % ROWS * 2 + column // ROWS).astype(jnp.float32)
    parted = parted.astype(jnp.bfloat16)
    plain = (row == column)[:ROWS, :ROWS].astype(jnp.float32).astype(jnp.bfloat16)

    def turned(value, order):
        return lax.dot_general(
            value, order, (((0,), (0,)), ((), ())), preferred_element_type=jnp.float32
        ).astype(jnp.bfloat16)

    def send(part, lanes, value):
        rows = slice(part * GROUPS_HERE, (part + 1) * GROUPS_HERE)
        send_ref[:, rows, lanes] = value.reshape(BLOCKS, GROUPS_HERE, -1)

    for which in range(2):
        left, right = 2 * which, 2 * which + 1
        copies[left].wait()
        copies[right].wait()
        product = gates_ref[left].reshape(2 * ROWS, ROWS).astype(jnp.float32) * gates_ref[
            right
        ].reshape(2 * ROWS, ROWS).astype(jnp.float32)
        signal = turned(product.astype(jnp.bfloat16), parted)
        for member in range(2):
            send(
                member,
                slice(which * ROWS, (which + 1) * ROWS),
                signal[:, member * ROWS : (member + 1) * ROWS],
            )
    copies[-1].wait()
    taps = turned(held_taps_ref[...], plain)
    for half in range(2):
        send(half, slice(2 * ROWS, None), taps[:, half * HALF : (half + 1) * HALF])


def gated_chunks(out_gate, in_gate, values_in, filter_taps, out_cotangent):
    return pl.pallas_call(
        gate_kernel,
        out_shape=jax.ShapeDtypeStruct((BLOCKS, SIGNALS, 5 * HALF), jnp.bfloat16),
        in_specs=[pl.BlockSpec(memory_space=pltpu.HBM)] * 5,
        out_specs=pl.BlockSpec(memory_space=pltpu.VMEM),
        scratch_shapes=[
            pltpu.VMEM((4, ROWS, 2, ROWS), jnp.bfloat16),
            pltpu.VMEM((ROWS, ROWS), jnp.bfloat16),
            pltpu.SemaphoreType.DMA((5,)),
        ],
        compiler_params=pltpu.CompilerParams(vmem_limit_bytes=16 * 1024 * 1024),
        cost_estimate=pl.CostEstimate(
            flops=400_000_000, bytes_accessed=2_000_000, transcendentals=0
        ),
        name="gates",
    )(
        *(
            pltpu.with_memory_space_constraint(value, pltpu.HBM)
            for value in (out_gate, in_gate, values_in, filter_taps, out_cotangent)
        )
    )


def lag_kernel(returned_ref, lag_ref, done):
    copy = pltpu.make_async_copy(returned_ref.at[:, :, pl.ds(4 * HALF, HALF)], lag_ref, done)
    copy.start()
    copy.wait()


def lag_chunks(returned):
    return pl.pallas_call(
        lag_kernel,
        out_shape=jax.ShapeDtypeStruct((BLOCKS, SIGNALS, HALF), jnp.bfloat16),
        in_specs=[pl.BlockSpec(memory_space=pltpu.VMEM)],
        out_specs=pl.BlockSpec(memory_space=pl.ANY),
        scratch_shapes=[pltpu.SemaphoreType.DMA],
        compiler_params=pltpu.CompilerParams(vmem_limit_bytes=16 * 1024 * 1024),
        name="lags",
    )(returned)


def unchunks(received, member_count):
    return (
        received.reshape(BLOCKS, member_count, GROUPS_HERE, ROWS)
        .transpose(3, 1, 0, 2)
        .reshape(ROWS, member_count, BLOCKS * GROUPS_HERE)
        .astype(jnp.float32)
    )


def rounded(value):
    return lax.reduce_precision(value, exponent_bits=8, mantissa_bits=7)


def exchange(value, axis):
    return lax.all_to_all(value, axis, split_axis=0, concat_axis=0, tiled=True)


def local(out_gate, in_gate, values_in, filter_taps, skip_gain, out_cotangent):
    row_count, member_count, group_count = out_gate.shape
    chan_count = lax.axis_size("chan")
    outgoing = gated_chunks(out_gate, in_gate, values_in, filter_taps, out_cotangent)
    returned = exchange(spectral(exchange(outgoing, "seq")), "seq")
    lag_terms = exchange(lag_chunks(returned).reshape(chan_count, -1, SIGNALS, HALF), "chan")
    norm_factor = 1.0 / math.sqrt(BLOCKS * row_count * member_count * chan_count)
    lag_sum = jnp.sum(lag_terms.astype(jnp.float32), axis=0)
    grad_filter = (
        lag_sum.reshape(-1, 2, GROUPS_HERE, HALF).transpose(1, 3, 0, 2).reshape(row_count, -1)
        * norm_factor
    )
    mixed_in = rounded(in_gate.astype(jnp.float32) * values_in.astype(jnp.float32))
    conv_cot = rounded(out_cotangent.astype(jnp.float32) * out_gate.astype(jnp.float32))
    conv_out = unchunks(returned[:, :, : 2 * HALF], member_count)
    back_conv = unchunks(returned[:, :, 2 * HALF : 4 * HALF], member_count)
    before_gate = conv_out + skip_gain[None] * mixed_in
    mixed = (out_gate.astype(jnp.float32) * before_gate).astype(jnp.bfloat16)
    grad_out_gate = (out_cotangent.astype(jnp.float32) * before_gate).astype(jnp.bfloat16)
    back_in = back_conv + skip_gain[None] * conv_cot
    grad_in_gate = (back_in * values_in.astype(jnp.float32)).astype(jnp.bfloat16)
    grad_values = (back_in * in_gate.astype(jnp.float32)).astype(jnp.bfloat16)
    return (mixed, grad_out_gate, grad_in_gate, grad_values, grad_filter)


def solution(mesh):
    in_specs = (
        P("seq", "chan", None),
        P("seq", "chan", None),
        P("seq", "chan", None),
        P("seq", None),
        P("chan", None),
        P("seq", "chan", None),
    )
    out_specs = (
        P("seq", "chan", None),
        P("seq", "chan", None),
        P("seq", "chan", None),
        P("seq", "chan", None),
        P("seq", "chan"),
    )
    return jax.shard_map(local, mesh=mesh, in_specs=in_specs, out_specs=out_specs, check_vma=False)
```

```python
import functools
import math

import jax
import jax.numpy as jnp
import ml_dtypes
import numpy as np
from jax import lax
from jax.experimental import pallas as pl
from jax.experimental.pallas import tpu as pltpu
from jax.sharding import PartitionSpec as P

BLOCKS = 64
ROWS = 256
HALF = ROWS // 2
SIGNALS = 8
GROUPS_HERE = 4
KEPT = 64
TILE = 16
FULL = 2 * BLOCKS * ROWS


def split_table(table):
    high = table.astype(ml_dtypes.bfloat16)
    low = (table - high.astype(np.float64)).astype(ml_dtypes.bfloat16)
    return high, low


def tables():
    kept = np.arange(KEPT)[:, None]
    block = np.arange(BLOCKS)[None, :]
    coarse = 2 * math.pi * (((2 * kept + 1) * block) % (4 * BLOCKS)) / (4 * BLOCKS)
    paired = np.stack([np.cos(coarse), -np.sin(coarse)]).reshape(2, -1, TILE, BLOCKS)
    enter_high, enter_low = split_table(paired.swapaxes(0, 1).reshape(2 * KEPT, BLOCKS))
    enter = np.concatenate([enter_high, enter_low], axis=1)
    leave_high, leave_low = split_table(
        np.concatenate([np.cos(coarse.T), -np.sin(coarse.T)], axis=1) * (2.0 / FULL)
    )
    leave = np.concatenate(
        [
            np.concatenate([leave_high, leave_high], axis=1),
            np.concatenate([leave_low, np.zeros_like(leave_low)], axis=1),
        ]
    )
    row = np.arange(ROWS)[None, :]
    twist = 2 * math.pi * (kept + 0.5) * row / FULL
    turn_cos = np.cos(twist).astype(np.float32)
    turn_sin = np.sin(twist).astype(np.float32)
    fine = []
    for odd in (0, 1):
        angle = (
            2
            * math.pi
            * ((np.arange(HALF)[:, None] * (2 * np.arange(HALF)[None, :] + odd)) % ROWS)
            / ROWS
        )
        cos, sin = np.cos(angle), np.sin(angle)
        forth = np.concatenate(
            [np.concatenate([cos, -sin], axis=1), np.concatenate([sin, cos], axis=1)], axis=0
        )
        fine.append((split_table(forth), split_table(forth.T)))
    forth, back = (
        np.stack([np.concatenate([high, low, high]) for high, low in (pair[way] for pair in fine)])
        for way in (0, 1)
    )
    return enter, leave, turn_cos, turn_sin, forth, back


def mxu(left, right):
    return jnp.dot(left, right, preferred_element_type=jnp.float32)


def halves(value):
    high = value.astype(jnp.bfloat16)
    low = (value - high.astype(jnp.float32)).astype(jnp.bfloat16)
    return high, low


class Stages:
    def __init__(self, cos_ref, sin_ref, enter_ref, leave_ref, forth_ref, back_ref):
        self.cos_ref = cos_ref
        self.sin_ref = sin_ref
        self.enter_ref = enter_ref
        self.leave_ref = leave_ref
        self.forth_ref = forth_ref
        self.back_ref = back_ref

    def put(self, pair, odd, rows, real, imag):
        for part, value in enumerate((real, imag)):
            lanes = slice(part * HALF, (part + 1) * HALF)
            for ref, piece in zip(pair, halves(value)):
                ref[odd, rows, lanes] = piece

    def both(self, pair, matrix_ref, odd, rows):
        high = pair[0][odd, rows, :]
        return mxu(jnp.concatenate([pair[1][odd, rows, :], high, high], axis=1), matrix_ref[odd])

    def turns(self, tile):
        return self.cos_ref[tile : tile + TILE, :], self.sin_ref[tile : tile + TILE, :]

    def enter(self, taken, pair, start):
        first = mxu(self.enter_ref[...], jnp.concatenate([taken, taken], axis=0))
        for tile in range(0, KEPT, TILE):
            real = first[2 * tile : 2 * tile + TILE]
            imag = first[2 * tile + TILE : 2 * tile + 2 * TILE]
            turn_cos, turn_sin = self.turns(tile)
            turned_real = real * turn_cos + imag * turn_sin
            turned_imag = imag * turn_cos - real * turn_sin
            rows = slice(start + tile, start + tile + TILE)
            near_real, far_real = turned_real[:, :HALF], turned_real[:, HALF:]
            near_imag, far_imag = turned_imag[:, :HALF], turned_imag[:, HALF:]
            self.put(pair, 0, rows, near_real + far_real, near_imag + far_imag)
            self.put(pair, 1, rows, near_real - far_real, near_imag - far_imag)

    def forth(self, pair, spec_ref, rows):
        for odd in (0, 1):
            spec_ref[odd, rows, :] = self.both(pair, self.forth_ref, odd, rows)

    def back(self, pair, turn_ref, rows):
        for odd in (0, 1):
            turn_ref[odd, rows, :] = self.both(pair, self.back_ref, odd, rows)

    def leave(self, turn_ref, start):
        pieces = [[], [], [], []]
        for tile in range(0, KEPT, TILE):
            rows = slice(start + tile, start + tile + TILE)
            turn_cos, turn_sin = self.turns(tile)
            even, odd = turn_ref[0, rows, :], turn_ref[1, rows, :]
            near, far = even + odd, even - odd
            real = jnp.concatenate([near[:, :HALF], far[:, :HALF]], axis=1)
            imag = jnp.concatenate([near[:, HALF:], far[:, HALF:]], axis=1)
            real_high, real_low = halves(real * turn_cos - imag * turn_sin)
            imag_high, imag_low = halves(imag * turn_cos + real * turn_sin)
            for kept, piece in zip(pieces, (real_high, imag_high, real_low, imag_low)):
                kept.append(piece)
        result = mxu(self.leave_ref[...], jnp.concatenate(sum(pieces, []), axis=0))
        return result[:BLOCKS] + result[BLOCKS:]


MEMBERS = SIGNALS // GROUPS_HERE
PAIRS = 2 * MEMBERS
GROUP_ROWS = PAIRS * KEPT


def every(row):
    return pl.ds(row, BLOCKS, stride=SIGNALS)


def spread(wide_ref, lane, received):
    wide_ref[lane] = received.astype(jnp.float32).reshape(BLOCKS * SIGNALS, HALF)


def gather(wide_ref, lane):
    return wide_ref[lane].reshape(BLOCKS, SIGNALS, HALF).astype(jnp.bfloat16)


def places(group, item):
    which, member = divmod(item, MEMBERS)
    row = member * GROUPS_HERE + group
    return ((2 * which, row), (2 * which + 1, row))


def spot(group, item, offset=0, size=KEPT):
    start = (group * PAIRS + item) * KEPT + offset
    return slice(start, start + size)


def lag_kernel(
    recv_ref,
    enter_ref,
    leave_ref,
    cos_ref,
    sin_ref,
    forth_ref,
    back_ref,
    lag_ref,
    spec_ref,
    wide_ref,
    high_ref,
    low_ref,
    high_lag_ref,
    low_lag_ref,
    turn_ref,
    wide_lag_ref,
):
    stages = Stages(cos_ref, sin_ref, enter_ref, leave_ref, forth_ref, back_ref)
    pair, joined = (high_ref, low_ref), (high_lag_ref, low_lag_ref)
    for lane in range(4):
        spread(wide_ref, lane, recv_ref[:, :, lane * HALF : (lane + 1) * HALF])
    for group in range(GROUPS_HERE):
        for item in range(PAIRS):
            taken = jnp.concatenate(
                [wide_ref[lane, every(row), :] for lane, row in places(group, item)], axis=1
            ).astype(jnp.bfloat16)
            stages.enter(taken, pair, spot(group, item).start)
    for group in range(GROUPS_HERE):
        stages.forth(pair, spec_ref, slice(group * GROUP_ROWS, (group + 1) * GROUP_ROWS))
    for group in range(GROUPS_HERE):
        for odd in (0, 1):
            for tile in range(0, KEPT, TILE):
                real = imag = None
                for member in range(MEMBERS):
                    rows = spot(group, member, tile, TILE)
                    in_real, in_imag = spec_ref[odd, rows, :HALF], spec_ref[odd, rows, HALF:]
                    rows = spot(group, MEMBERS + member, tile, TILE)
                    cot_real, cot_imag = spec_ref[odd, rows, :HALF], spec_ref[odd, rows, HALF:]
                    more_real = cot_real * in_real + cot_imag * in_imag
                    more_imag = cot_imag * in_real - cot_real * in_imag
                    real = more_real if member == 0 else real + more_real
                    imag = more_imag if member == 0 else imag + more_imag
                start = group * KEPT + tile
                stages.put(joined, odd, slice(start, start + TILE), real, imag)
    stages.back(joined, turn_ref, slice(0, GROUPS_HERE * KEPT))
    for group in range(GROUPS_HERE):
        result = stages.leave(turn_ref, group * KEPT)
        wide_lag_ref[0, every(group), :] = result[:, :HALF]
        wide_lag_ref[0, every(group + GROUPS_HERE), :] = result[:, HALF:]
    lag_ref[...] = gather(wide_lag_ref, 0)


def signal_kernel(
    plane_ref,
    skip_ref,
    recv_ref,
    spec_ref,
    wide_ref,
    enter_ref,
    leave_ref,
    cos_ref,
    sin_ref,
    forth_ref,
    back_ref,
    send_ref,
    wide_taps_ref,
    high_taps_ref,
    low_taps_ref,
    spec_taps_ref,
    high_ref,
    low_ref,
    turn_ref,
    wide_out_ref,
):
    stages = Stages(cos_ref, sin_ref, enter_ref, leave_ref, forth_ref, back_ref)
    taps_pair, pair = (high_taps_ref, low_taps_ref), (high_ref, low_ref)
    first_group = plane_ref[1] * GROUPS_HERE
    spread(wide_taps_ref, 0, recv_ref[:, :, 4 * HALF :])
    for group in range(GROUPS_HERE):
        taken = jnp.concatenate(
            [
                wide_taps_ref[0, every(group), :],
                wide_taps_ref[0, every(group + GROUPS_HERE), :],
            ],
            axis=1,
        ).astype(jnp.bfloat16)
        stages.enter(taken, taps_pair, group * KEPT)
    stages.forth(taps_pair, spec_taps_ref, slice(0, GROUPS_HERE * KEPT))

    def multiply(group):
        for odd in (0, 1):
            for tile in range(0, KEPT, TILE):
                rows = slice(group * KEPT + tile, group * KEPT + tile + TILE)
                tap_real, tap_imag = spec_taps_ref[odd, rows, :HALF], spec_taps_ref[odd, rows, HALF:]
                for item in range(PAIRS):
                    rows = spot(group, item, tile, TILE)
                    real, imag = spec_ref[odd, rows, :HALF], spec_ref[odd, rows, HALF:]
                    turn = tap_imag if item < MEMBERS else -tap_imag
                    stages.put(
                        pair,
                        odd,
                        rows,
                        real * tap_real - imag * turn,
                        real * turn + imag * tap_real,
                    )

    def back(group):
        stages.back(pair, turn_ref, slice(group * GROUP_ROWS, (group + 1) * GROUP_ROWS))

    def leave(group):
        for item in range(PAIRS):
            result = stages.leave(turn_ref, spot(group, item).start)
            gain = skip_ref[item % MEMBERS, first_group + group]
            for part, (lane, row) in enumerate(places(group, item)):
                direct = wide_ref[lane, every(row), :] * gain
                wide_out_ref[lane, every(row), :] = (
                    result[:, part * HALF : (part + 1) * HALF] + direct
                )

    for step in range(GROUPS_HERE + 2):
        for lag, stage in enumerate((multiply, back, leave)):
            if 0 <= step - lag < GROUPS_HERE:
                stage(step - lag)
    for lane in range(4):
        send_ref[:, :, lane * HALF : (lane + 1) * HALF] = gather(wide_out_ref, lane)


def spectral(received, plane, skip_gain, send_lag):
    constants = [jnp.asarray(table) for table in tables()]
    signal_rows, group_rows = GROUPS_HERE * GROUP_ROWS, GROUPS_HERE * KEPT
    whole = pl.BlockSpec(memory_space=pltpu.VMEM)
    scalar = pl.BlockSpec(memory_space=pltpu.SMEM)
    params = pltpu.CompilerParams(vmem_limit_bytes=24 * 1024 * 1024)
    lag, spec, wide = pl.pallas_call(
        lag_kernel,
        out_shape=(
            jax.ShapeDtypeStruct((BLOCKS, SIGNALS, HALF), jnp.bfloat16),
            jax.ShapeDtypeStruct((2, signal_rows, ROWS), jnp.float32),
            jax.ShapeDtypeStruct((4, BLOCKS * SIGNALS, HALF), jnp.float32),
        ),
        in_specs=[whole] * 7,
        out_specs=(whole,) * 3,
        scratch_shapes=[
            pltpu.VMEM((2, signal_rows, ROWS), jnp.bfloat16),
            pltpu.VMEM((2, signal_rows, ROWS), jnp.bfloat16),
            pltpu.VMEM((2, group_rows, ROWS), jnp.bfloat16),
            pltpu.VMEM((2, group_rows, ROWS), jnp.bfloat16),
            pltpu.VMEM((2, group_rows, ROWS), jnp.float32),
            pltpu.VMEM((1, BLOCKS * SIGNALS, HALF), jnp.float32),
        ],
        compiler_params=params,
        cost_estimate=pl.CostEstimate(
            flops=3_000_000_000, bytes_accessed=5_000_000, transcendentals=0
        ),
        name="lags",
    )(received, *constants)
    moved = send_lag(lag)
    signals = pl.pallas_call(
        signal_kernel,
        out_shape=jax.ShapeDtypeStruct((BLOCKS, SIGNALS, 4 * HALF), jnp.bfloat16),
        in_specs=[scalar] * 2 + [whole] * 9,
        out_specs=whole,
        scratch_shapes=[
            pltpu.VMEM((1, BLOCKS * SIGNALS, HALF), jnp.float32),
            pltpu.VMEM((2, group_rows, ROWS), jnp.bfloat16),
            pltpu.VMEM((2, group_rows, ROWS), jnp.bfloat16),
            pltpu.VMEM((2, group_rows, ROWS), jnp.float32),
            pltpu.VMEM((2, signal_rows, ROWS), jnp.bfloat16),
            pltpu.VMEM((2, signal_rows, ROWS), jnp.bfloat16),
            pltpu.VMEM((2, signal_rows, ROWS), jnp.float32),
            pltpu.VMEM((4, BLOCKS * SIGNALS, HALF), jnp.float32),
        ],
        compiler_params=params,
        cost_estimate=pl.CostEstimate(
            flops=3_000_000_000, bytes_accessed=5_000_000, transcendentals=0
        ),
        name="signals",
    )(plane, skip_gain, received, spec, wide, *constants)
    return jnp.concatenate([signals, moved], axis=2)


RING = 8


def shift(row, column):
    return (row + RING // 2 * (column % 2)) % RING


def holders(plane):
    return [
        [lax.rem(first - RING // 2 * odd + 2 * RING - plane, RING) for odd in (0, 1)]
        for first in range(RING)
    ]


def gate_kernel(
    plane_ref,
    out_gate_ref,
    in_gate_ref,
    values_ref,
    taps_ref,
    cot_ref,
    send_ref,
    gates_ref,
    held_taps_ref,
    arrived,
):
    sources = (in_gate_ref, values_ref, cot_ref, out_gate_ref)
    copies = [
        pltpu.make_async_copy(source, gates_ref.at[slot], arrived.at[slot])
        for slot, source in enumerate(sources)
    ]
    copies.append(pltpu.make_async_copy(taps_ref, held_taps_ref, arrived.at[len(sources)]))
    for copy in copies:
        copy.start()

    row = lax.broadcasted_iota(jnp.int32, (2 * ROWS, 2 * ROWS), 0)
    column = lax.broadcasted_iota(jnp.int32, (2 * ROWS, 2 * ROWS), 1)
    parted = (row == column % ROWS * 2 + column // ROWS).astype(jnp.float32)
    parted = parted.astype(jnp.bfloat16)
    plain = (row == column)[:ROWS, :ROWS].astype(jnp.float32).astype(jnp.bfloat16)

    def turned(value, order):
        return lax.dot_general(
            value, order, (((0,), (0,)), ((), ())), preferred_element_type=jnp.float32
        ).astype(jnp.bfloat16)

    owners = holders(plane_ref[0])

    def send(part, lanes, value):
        rows = slice(part * GROUPS_HERE, (part + 1) * GROUPS_HERE)
        value = value.reshape(BLOCKS, GROUPS_HERE, -1)
        for first in range(RING):
            for second in range(RING):
                send_ref[owners[first][second % 2], second, rows, lanes] = value[
                    first * RING + second
                ]

    for which in range(2):
        left, right = 2 * which, 2 * which + 1
        copies[left].wait()
        copies[right].wait()
        product = gates_ref[left].reshape(2 * ROWS, ROWS).astype(jnp.float32) * gates_ref[
            right
        ].reshape(2 * ROWS, ROWS).astype(jnp.float32)
        signal = turned(product.astype(jnp.bfloat16), parted)
        for member in range(2):
            send(
                member,
                slice(which * ROWS, (which + 1) * ROWS),
                signal[:, member * ROWS : (member + 1) * ROWS],
            )
    copies[-1].wait()
    taps = turned(held_taps_ref[...], plain)
    for half in range(2):
        send(half, slice(2 * ROWS, None), taps[:, half * HALF : (half + 1) * HALF])


def gated_chunks(plane, out_gate, in_gate, values_in, filter_taps, out_cotangent):
    return pl.pallas_call(
        gate_kernel,
        out_shape=jax.ShapeDtypeStruct((RING, RING, SIGNALS, 5 * HALF), jnp.bfloat16),
        in_specs=[pl.BlockSpec(memory_space=pltpu.SMEM)]
        + [pl.BlockSpec(memory_space=pltpu.HBM)] * 5,
        out_specs=pl.BlockSpec(memory_space=pltpu.VMEM),
        scratch_shapes=[
            pltpu.VMEM((4, ROWS, 2, ROWS), jnp.bfloat16),
            pltpu.VMEM((ROWS, ROWS), jnp.bfloat16),
            pltpu.SemaphoreType.DMA((5,)),
        ],
        compiler_params=pltpu.CompilerParams(vmem_limit_bytes=16 * 1024 * 1024),
        cost_estimate=pl.CostEstimate(
            flops=400_000_000, bytes_accessed=2_000_000, transcendentals=0
        ),
        name="gates",
    )(
        plane,
        *(
            pltpu.with_memory_space_constraint(value, pltpu.HBM)
            for value in (out_gate, in_gate, values_in, filter_taps, out_cotangent)
        )
    )


def outcome_kernel(
    scale,
    plane_ref,
    returned_ref,
    out_gate_ref,
    in_gate_ref,
    values_ref,
    cot_ref,
    mixed_ref,
    grad_out_gate_ref,
    grad_in_gate_ref,
    grad_values_ref,
    grad_filter_ref,
    ordered_ref,
    results_ref,
    sums_ref,
    left,
):
    owners = holders(plane_ref[0])
    for first in range(RING):
        for second in range(RING):
            ordered_ref[first * RING + second] = returned_ref[
                owners[first][second % 2], second, :, : 2 * ROWS
            ]
    row = lax.broadcasted_iota(jnp.int32, (2 * ROWS, 2 * ROWS), 0)
    column = lax.broadcasted_iota(jnp.int32, (2 * ROWS, 2 * ROWS), 1)
    parted = (column == row % 2 * ROWS + row // 2).astype(jnp.float32).astype(jnp.bfloat16)
    copies = []
    results = (
        (mixed_ref, out_gate_ref),
        (grad_out_gate_ref, cot_ref),
        (grad_in_gate_ref, values_ref),
        (grad_values_ref, in_gate_ref),
    )
    for which in range(2):
        lanes = slice(which * ROWS, (which + 1) * ROWS)
        turned = jnp.concatenate(
            [
                ordered_ref[:, part * GROUPS_HERE : (part + 1) * GROUPS_HERE, lanes].reshape(
                    ROWS, ROWS
                )
                for part in range(2)
            ],
            axis=1,
        )
        signal = lax.dot_general(
            parted, turned, (((1,), (1,)), ((), ())), preferred_element_type=jnp.float32
        )
        for slot in (2 * which, 2 * which + 1):
            result_ref, gate_ref = results[slot]
            gate = gate_ref[...].reshape(2 * ROWS, ROWS).astype(jnp.float32)
            results_ref[slot] = (signal * gate).astype(jnp.bfloat16).reshape(ROWS, 2, ROWS)
            copies.append(
                pltpu.make_async_copy(results_ref.at[slot], result_ref, left.at[slot])
            )
            copies[-1].start()
    for second in range(RING):
        total = returned_ref[0, second, :, 2 * ROWS :].astype(jnp.float32)
        for first in range(1, RING):
            total += returned_ref[first, second, :, 2 * ROWS :].astype(jnp.float32)
        total = total * scale
        rows = slice(second * GROUPS_HERE, (second + 1) * GROUPS_HERE)
        sums_ref[rows, :HALF] = total[:GROUPS_HERE]
        sums_ref[rows, HALF:] = total[GROUPS_HERE:]
    copies.append(pltpu.make_async_copy(sums_ref, grad_filter_ref, left.at[len(results)]))
    copies[-1].start()
    for copy in copies:
        copy.wait()


def outcomes(scale, plane, returned, out_gate, in_gate, values_in, out_cotangent):
    whole = pl.BlockSpec(memory_space=pltpu.VMEM)
    signal = jax.ShapeDtypeStruct((ROWS, 2, ROWS), jnp.bfloat16)
    return pl.pallas_call(
        functools.partial(outcome_kernel, scale),
        out_shape=(signal,) * 4
        + (jax.ShapeDtypeStruct((RING * GROUPS_HERE, ROWS), jnp.float32),),
        in_specs=[pl.BlockSpec(memory_space=pltpu.SMEM)] + [whole] * 5,
        out_specs=(pl.BlockSpec(memory_space=pl.ANY),) * 5,
        scratch_shapes=[
            pltpu.VMEM((BLOCKS, SIGNALS, 2 * ROWS), jnp.bfloat16),
            pltpu.VMEM((4, ROWS, 2, ROWS), jnp.bfloat16),
            pltpu.VMEM((RING * GROUPS_HERE, ROWS), jnp.float32),
            pltpu.SemaphoreType.DMA((5,)),
        ],
        compiler_params=pltpu.CompilerParams(vmem_limit_bytes=16 * 1024 * 1024),
        cost_estimate=pl.CostEstimate(
            flops=400_000_000, bytes_accessed=3_000_000, transcendentals=0
        ),
        name="outcomes",
    )(plane, returned, out_gate, in_gate, values_in, out_cotangent)


def exchange(value, axis):
    return lax.all_to_all(value, axis, split_axis=0, concat_axis=0, tiled=True)


def local(out_gate, in_gate, values_in, filter_taps, skip_gain, out_cotangent):
    row_count, member_count, group_count = out_gate.shape
    chan_count = lax.axis_size("chan")
    plane = lax.axis_index("chan")
    row, column = jnp.divmod(lax.axis_index("seq"), RING)
    owned = (plane + shift(row, column)) % RING * RING + column
    plane = jnp.stack([plane, owned]).astype(jnp.int32)

    def send_lag(lag):
        pairs = [
            (
                (first * RING + second) * RING + level,
                (first * RING + second) * RING + (level + shift(first, second)) % RING,
            )
            for first in range(RING)
            for second in range(RING)
            for level in range(RING)
        ]
        return lax.ppermute(lag, ("seq", "chan"), pairs)

    outgoing = gated_chunks(plane, out_gate, in_gate, values_in, filter_taps, out_cotangent)
    received = exchange(outgoing.reshape(BLOCKS, SIGNALS, 5 * HALF), "seq")
    returned = exchange(spectral(received, plane, skip_gain, send_lag), "seq")
    norm_factor = 1.0 / math.sqrt(BLOCKS * row_count * member_count * chan_count)
    *gradients, filter_sum = outcomes(
        norm_factor,
        plane,
        returned.reshape(RING, RING, SIGNALS, 5 * HALF),
        out_gate,
        in_gate,
        values_in,
        out_cotangent,
    )
    return (*gradients, filter_sum.T)


def solution(mesh):
    in_specs = (
        P("seq", "chan", None),
        P("seq", "chan", None),
        P("seq", "chan", None),
        P("seq", None),
        P("chan", None),
        P("seq", "chan", None),
    )
    out_specs = (
        P("seq", "chan", None),
        P("seq", "chan", None),
        P("seq", "chan", None),
        P("seq", "chan", None),
        P("seq", "chan"),
    )
    return jax.shard_map(local, mesh=mesh, in_specs=in_specs, out_specs=out_specs, check_vma=False)
```

```python
import functools
import math

import jax
import jax.numpy as jnp
import ml_dtypes
import numpy as np
from jax import lax
from jax.experimental import pallas as pl
from jax.experimental.pallas import tpu as pltpu
from jax.sharding import PartitionSpec as P

BLOCKS = 64
ROWS = 256
HALF = ROWS // 2
SIGNALS = 8
GROUPS_HERE = 4
KEPT = 64
TILE = 16
FULL = 2 * BLOCKS * ROWS


def split_table(table):
    high = table.astype(ml_dtypes.bfloat16)
    low = (table - high.astype(np.float64)).astype(ml_dtypes.bfloat16)
    return high, low


def tables():
    kept = np.arange(KEPT)[:, None]
    block = np.arange(BLOCKS)[None, :]
    coarse = 2 * math.pi * (((2 * kept + 1) * block) % (4 * BLOCKS)) / (4 * BLOCKS)
    paired = np.stack([np.cos(coarse), -np.sin(coarse)]).reshape(2, -1, TILE, BLOCKS)
    enter_high, enter_low = split_table(paired.swapaxes(0, 1).reshape(2 * KEPT, BLOCKS))
    enter = np.concatenate([enter_high, enter_low], axis=1)
    leave_high, leave_low = split_table(
        np.concatenate([np.cos(coarse.T), -np.sin(coarse.T)], axis=1) * (2.0 / FULL)
    )
    leave = np.concatenate(
        [
            np.concatenate([leave_high, leave_high], axis=1),
            np.concatenate([leave_low, np.zeros_like(leave_low)], axis=1),
        ]
    )
    row = np.arange(ROWS)[None, :]
    twist = 2 * math.pi * (kept + 0.5) * row / FULL
    turn_cos = np.cos(twist).astype(np.float32)
    turn_sin = np.sin(twist).astype(np.float32)
    fine = []
    for odd in (0, 1):
        angle = (
            2
            * math.pi
            * ((np.arange(HALF)[:, None] * (2 * np.arange(HALF)[None, :] + odd)) % ROWS)
            / ROWS
        )
        cos, sin = np.cos(angle), np.sin(angle)
        forth = np.concatenate(
            [np.concatenate([cos, -sin], axis=1), np.concatenate([sin, cos], axis=1)], axis=0
        )
        fine.append((split_table(forth), split_table(forth.T)))
    forth, back = (
        np.stack([np.concatenate([high, low, high]) for high, low in (pair[way] for pair in fine)])
        for way in (0, 1)
    )
    return enter, leave, turn_cos, turn_sin, forth, back


def mxu(left, right):
    return jnp.dot(left, right, preferred_element_type=jnp.float32)


def halves(value):
    high = value.astype(jnp.bfloat16)
    low = (value - high.astype(jnp.float32)).astype(jnp.bfloat16)
    return high, low


class Stages:
    def __init__(self, cos_ref, sin_ref, enter_ref, leave_ref, forth_ref, back_ref):
        self.cos_ref = cos_ref
        self.sin_ref = sin_ref
        self.enter_ref = enter_ref
        self.leave_ref = leave_ref
        self.forth_ref = forth_ref
        self.back_ref = back_ref

    def put(self, pair, odd, rows, real, imag):
        for part, value in enumerate((real, imag)):
            lanes = slice(part * HALF, (part + 1) * HALF)
            for ref, piece in zip(pair, halves(value)):
                ref[odd, rows, lanes] = piece

    def both(self, pair, matrix_ref, odd, rows):
        high = pair[0][odd, rows, :]
        return mxu(jnp.concatenate([pair[1][odd, rows, :], high, high], axis=1), matrix_ref[odd])

    def turns(self, tile):
        return self.cos_ref[tile : tile + TILE, :], self.sin_ref[tile : tile + TILE, :]

    def enter(self, taken, pair, start):
        first = mxu(self.enter_ref[...], jnp.concatenate([taken, taken], axis=0))
        for tile in range(0, KEPT, TILE):
            real = first[2 * tile : 2 * tile + TILE]
            imag = first[2 * tile + TILE : 2 * tile + 2 * TILE]
            turn_cos, turn_sin = self.turns(tile)
            turned_real = real * turn_cos + imag * turn_sin
            turned_imag = imag * turn_cos - real * turn_sin
            rows = slice(start + tile, start + tile + TILE)
            near_real, far_real = turned_real[:, :HALF], turned_real[:, HALF:]
            near_imag, far_imag = turned_imag[:, :HALF], turned_imag[:, HALF:]
            self.put(pair, 0, rows, near_real + far_real, near_imag + far_imag)
            self.put(pair, 1, rows, near_real - far_real, near_imag - far_imag)

    def forth(self, pair, spec_ref, rows):
        for odd in (0, 1):
            spec_ref[odd, rows, :] = self.both(pair, self.forth_ref, odd, rows)

    def back(self, pair, turn_ref, rows):
        for odd in (0, 1):
            turn_ref[odd, rows, :] = self.both(pair, self.back_ref, odd, rows)

    def leave(self, turn_ref, start):
        pieces = [[], [], [], []]
        for tile in range(0, KEPT, TILE):
            rows = slice(start + tile, start + tile + TILE)
            turn_cos, turn_sin = self.turns(tile)
            even, odd = turn_ref[0, rows, :], turn_ref[1, rows, :]
            near, far = even + odd, even - odd
            real = jnp.concatenate([near[:, :HALF], far[:, :HALF]], axis=1)
            imag = jnp.concatenate([near[:, HALF:], far[:, HALF:]], axis=1)
            real_high, real_low = halves(real * turn_cos - imag * turn_sin)
            imag_high, imag_low = halves(imag * turn_cos + real * turn_sin)
            for kept, piece in zip(pieces, (real_high, imag_high, real_low, imag_low)):
                kept.append(piece)
        result = mxu(self.leave_ref[...], jnp.concatenate(sum(pieces, []), axis=0))
        return result[:BLOCKS] + result[BLOCKS:]


MEMBERS = SIGNALS // GROUPS_HERE
PAIRS = 2 * MEMBERS
GROUP_ROWS = PAIRS * KEPT


def every(row):
    return pl.ds(row, BLOCKS, stride=SIGNALS)


def spread(wide_ref, lane, received):
    wide_ref[lane] = received.astype(jnp.float32).reshape(BLOCKS * SIGNALS, HALF)


def gather(wide_ref, lane):
    return wide_ref[lane].reshape(BLOCKS, SIGNALS, HALF).astype(jnp.bfloat16)


def places(group, item):
    which, member = divmod(item, MEMBERS)
    row = member * GROUPS_HERE + group
    return ((2 * which, row), (2 * which + 1, row))


def spot(group, item, offset=0, size=KEPT):
    start = (group * PAIRS + item) * KEPT + offset
    return slice(start, start + size)


def lag_kernel(
    recv_ref,
    enter_ref,
    leave_ref,
    cos_ref,
    sin_ref,
    forth_ref,
    back_ref,
    lag_ref,
    spec_ref,
    wide_ref,
    high_ref,
    low_ref,
    high_lag_ref,
    low_lag_ref,
    turn_ref,
    wide_lag_ref,
):
    stages = Stages(cos_ref, sin_ref, enter_ref, leave_ref, forth_ref, back_ref)
    pair, joined = (high_ref, low_ref), (high_lag_ref, low_lag_ref)
    for lane in range(4):
        spread(wide_ref, lane, recv_ref[:, :, lane * HALF : (lane + 1) * HALF])
    for group in range(GROUPS_HERE):
        for item in range(PAIRS):
            taken = jnp.concatenate(
                [wide_ref[lane, every(row), :] for lane, row in places(group, item)], axis=1
            ).astype(jnp.bfloat16)
            stages.enter(taken, pair, spot(group, item).start)
    for group in range(GROUPS_HERE):
        stages.forth(pair, spec_ref, slice(group * GROUP_ROWS, (group + 1) * GROUP_ROWS))
    for group in range(GROUPS_HERE):
        for odd in (0, 1):
            for tile in range(0, KEPT, TILE):
                real = imag = None
                for member in range(MEMBERS):
                    rows = spot(group, member, tile, TILE)
                    in_real, in_imag = spec_ref[odd, rows, :HALF], spec_ref[odd, rows, HALF:]
                    rows = spot(group, MEMBERS + member, tile, TILE)
                    cot_real, cot_imag = spec_ref[odd, rows, :HALF], spec_ref[odd, rows, HALF:]
                    more_real = cot_real * in_real + cot_imag * in_imag
                    more_imag = cot_imag * in_real - cot_real * in_imag
                    real = more_real if member == 0 else real + more_real
                    imag = more_imag if member == 0 else imag + more_imag
                start = group * KEPT + tile
                stages.put(joined, odd, slice(start, start + TILE), real, imag)
    stages.back(joined, turn_ref, slice(0, GROUPS_HERE * KEPT))
    for group in range(GROUPS_HERE):
        result = stages.leave(turn_ref, group * KEPT)
        wide_lag_ref[0, every(group), :] = result[:, :HALF]
        wide_lag_ref[0, every(group + GROUPS_HERE), :] = result[:, HALF:]
    lag_ref[...] = gather(wide_lag_ref, 0)


def signal_kernel(
    skip_ref,
    recv_ref,
    spec_ref,
    wide_ref,
    enter_ref,
    leave_ref,
    cos_ref,
    sin_ref,
    forth_ref,
    back_ref,
    send_ref,
    wide_taps_ref,
    high_taps_ref,
    low_taps_ref,
    spec_taps_ref,
    high_ref,
    low_ref,
    turn_ref,
    wide_out_ref,
):
    stages = Stages(cos_ref, sin_ref, enter_ref, leave_ref, forth_ref, back_ref)
    taps_pair, pair = (high_taps_ref, low_taps_ref), (high_ref, low_ref)
    skip = jnp.concatenate([skip_ref[...], jnp.zeros((6, ROWS), jnp.float32)], axis=0)
    gains = pltpu.roll(skip, lax.rem(ROWS - position()[1] * GROUPS_HERE, ROWS), 1)
    spread(wide_taps_ref, 0, recv_ref[:, :, 4 * HALF :])
    for group in range(GROUPS_HERE):
        taken = jnp.concatenate(
            [
                wide_taps_ref[0, every(group), :],
                wide_taps_ref[0, every(group + GROUPS_HERE), :],
            ],
            axis=1,
        ).astype(jnp.bfloat16)
        stages.enter(taken, taps_pair, group * KEPT)
    stages.forth(taps_pair, spec_taps_ref, slice(0, GROUPS_HERE * KEPT))

    def multiply(group):
        for odd in (0, 1):
            for tile in range(0, KEPT, TILE):
                rows = slice(group * KEPT + tile, group * KEPT + tile + TILE)
                tap_real, tap_imag = spec_taps_ref[odd, rows, :HALF], spec_taps_ref[odd, rows, HALF:]
                for item in range(PAIRS):
                    rows = spot(group, item, tile, TILE)
                    real, imag = spec_ref[odd, rows, :HALF], spec_ref[odd, rows, HALF:]
                    turn = tap_imag if item < MEMBERS else -tap_imag
                    stages.put(
                        pair,
                        odd,
                        rows,
                        real * tap_real - imag * turn,
                        real * turn + imag * tap_real,
                    )

    def back(group):
        stages.back(pair, turn_ref, slice(group * GROUP_ROWS, (group + 1) * GROUP_ROWS))

    def leave(group):
        for item in range(PAIRS):
            result = stages.leave(turn_ref, spot(group, item).start)
            member = item % MEMBERS
            gain = gains[member : member + 1, group : group + 1]
            for part, (lane, row) in enumerate(places(group, item)):
                direct = wide_ref[lane, every(row), :] * gain
                wide_out_ref[lane, every(row), :] = (
                    result[:, part * HALF : (part + 1) * HALF] + direct
                )

    for step in range(GROUPS_HERE + 2):
        for lag, stage in enumerate((multiply, back, leave)):
            if 0 <= step - lag < GROUPS_HERE:
                stage(step - lag)
    for lane in range(4):
        send_ref[:, :, lane * HALF : (lane + 1) * HALF] = gather(wide_out_ref, lane)


def spectral(received, skip_gain, send_lag):
    constants = [jnp.asarray(table) for table in tables()]
    signal_rows, group_rows = GROUPS_HERE * GROUP_ROWS, GROUPS_HERE * KEPT
    whole = pl.BlockSpec(memory_space=pltpu.VMEM)
    params = pltpu.CompilerParams(vmem_limit_bytes=24 * 1024 * 1024)
    lag, spec, wide = pl.pallas_call(
        lag_kernel,
        out_shape=(
            jax.ShapeDtypeStruct((BLOCKS, SIGNALS, HALF), jnp.bfloat16),
            jax.ShapeDtypeStruct((2, signal_rows, ROWS), jnp.float32),
            jax.ShapeDtypeStruct((4, BLOCKS * SIGNALS, HALF), jnp.float32),
        ),
        in_specs=[whole] * 7,
        out_specs=(whole,) * 3,
        scratch_shapes=[
            pltpu.VMEM((2, signal_rows, ROWS), jnp.bfloat16),
            pltpu.VMEM((2, signal_rows, ROWS), jnp.bfloat16),
            pltpu.VMEM((2, group_rows, ROWS), jnp.bfloat16),
            pltpu.VMEM((2, group_rows, ROWS), jnp.bfloat16),
            pltpu.VMEM((2, group_rows, ROWS), jnp.float32),
            pltpu.VMEM((1, BLOCKS * SIGNALS, HALF), jnp.float32),
        ],
        compiler_params=params,
        cost_estimate=pl.CostEstimate(
            flops=3_000_000_000, bytes_accessed=5_000_000, transcendentals=0
        ),
        name="lags",
    )(received, *constants)
    moved = send_lag(lag)
    signals = pl.pallas_call(
        signal_kernel,
        out_shape=jax.ShapeDtypeStruct((BLOCKS, SIGNALS, 4 * HALF), jnp.bfloat16),
        in_specs=[whole] * 10,
        out_specs=whole,
        scratch_shapes=[
            pltpu.VMEM((1, BLOCKS * SIGNALS, HALF), jnp.float32),
            pltpu.VMEM((2, group_rows, ROWS), jnp.bfloat16),
            pltpu.VMEM((2, group_rows, ROWS), jnp.bfloat16),
            pltpu.VMEM((2, group_rows, ROWS), jnp.float32),
            pltpu.VMEM((2, signal_rows, ROWS), jnp.bfloat16),
            pltpu.VMEM((2, signal_rows, ROWS), jnp.bfloat16),
            pltpu.VMEM((2, signal_rows, ROWS), jnp.float32),
            pltpu.VMEM((4, BLOCKS * SIGNALS, HALF), jnp.float32),
        ],
        compiler_params=params,
        cost_estimate=pl.CostEstimate(
            flops=3_000_000_000, bytes_accessed=5_000_000, transcendentals=0
        ),
        name="signals",
    )(skip_gain, received, spec, wide, *constants)
    return jnp.concatenate([signals, moved], axis=2)


RING = 8


def shift(row, column):
    return (row + RING // 2 * (column % 2)) % RING


def position():
    seat, plane = lax.axis_index("seq"), lax.axis_index("chan")
    row, column = lax.div(seat, RING), lax.rem(seat, RING)
    held = lax.rem(plane + row + RING // 2 * lax.rem(column, 2), RING) * RING + column
    return plane, held


def holders(plane):
    return [
        [lax.rem(first - RING // 2 * odd + 2 * RING - plane, RING) for odd in (0, 1)]
        for first in range(RING)
    ]


def gate_kernel(
    out_gate_ref,
    in_gate_ref,
    values_ref,
    taps_ref,
    cot_ref,
    send_ref,
    gates_ref,
    held_taps_ref,
    arrived,
):
    sources = (in_gate_ref, values_ref, cot_ref, out_gate_ref)
    copies = [
        pltpu.make_async_copy(source, gates_ref.at[slot], arrived.at[slot])
        for slot, source in enumerate(sources)
    ]
    copies.append(pltpu.make_async_copy(taps_ref, held_taps_ref, arrived.at[len(sources)]))
    for copy in copies:
        copy.start()

    row = lax.broadcasted_iota(jnp.int32, (2 * ROWS, 2 * ROWS), 0)
    column = lax.broadcasted_iota(jnp.int32, (2 * ROWS, 2 * ROWS), 1)
    parted = (row == column % ROWS * 2 + column // ROWS).astype(jnp.float32)
    parted = parted.astype(jnp.bfloat16)
    plain = (row == column)[:ROWS, :ROWS].astype(jnp.float32).astype(jnp.bfloat16)

    def turned(value, order):
        return lax.dot_general(
            value, order, (((0,), (0,)), ((), ())), preferred_element_type=jnp.float32
        ).astype(jnp.bfloat16)

    owners = holders(position()[0])

    def send(part, lanes, value):
        rows = slice(part * GROUPS_HERE, (part + 1) * GROUPS_HERE)
        value = value.reshape(BLOCKS, GROUPS_HERE, -1)
        for first in range(RING):
            for second in range(RING):
                send_ref[owners[first][second % 2], second, rows, lanes] = value[
                    first * RING + second
                ]

    for which in range(2):
        left, right = 2 * which, 2 * which + 1
        copies[left].wait()
        copies[right].wait()
        product = gates_ref[left].reshape(2 * ROWS, ROWS).astype(jnp.float32) * gates_ref[
            right
        ].reshape(2 * ROWS, ROWS).astype(jnp.float32)
        signal = turned(product.astype(jnp.bfloat16), parted)
        for member in range(2):
            send(
                member,
                slice(which * ROWS, (which + 1) * ROWS),
                signal[:, member * ROWS : (member + 1) * ROWS],
            )
    copies[-1].wait()
    taps = turned(held_taps_ref[...], plain)
    for half in range(2):
        send(half, slice(2 * ROWS, None), taps[:, half * HALF : (half + 1) * HALF])


def gated_chunks(out_gate, in_gate, values_in, filter_taps, out_cotangent):
    return pl.pallas_call(
        gate_kernel,
        out_shape=jax.ShapeDtypeStruct((RING, RING, SIGNALS, 5 * HALF), jnp.bfloat16),
        in_specs=[pl.BlockSpec(memory_space=pltpu.HBM)] * 5,
        out_specs=pl.BlockSpec(memory_space=pltpu.VMEM),
        scratch_shapes=[
            pltpu.VMEM((4, ROWS, 2, ROWS), jnp.bfloat16),
            pltpu.VMEM((ROWS, ROWS), jnp.bfloat16),
            pltpu.SemaphoreType.DMA((5,)),
        ],
        compiler_params=pltpu.CompilerParams(vmem_limit_bytes=16 * 1024 * 1024),
        cost_estimate=pl.CostEstimate(
            flops=400_000_000, bytes_accessed=2_000_000, transcendentals=0
        ),
        name="gates",
    )(
        *(
            pltpu.with_memory_space_constraint(value, pltpu.HBM)
            for value in (out_gate, in_gate, values_in, filter_taps, out_cotangent)
        )
    )


def outcome_kernel(
    scale,
    returned_ref,
    out_gate_ref,
    in_gate_ref,
    values_ref,
    cot_ref,
    mixed_ref,
    grad_out_gate_ref,
    grad_in_gate_ref,
    grad_values_ref,
    grad_filter_ref,
    ordered_ref,
    results_ref,
    sums_ref,
    left,
):
    owners = holders(position()[0])
    for first in range(RING):
        for second in range(RING):
            ordered_ref[first * RING + second] = returned_ref[
                owners[first][second % 2], second, :, : 2 * ROWS
            ]
    row = lax.broadcasted_iota(jnp.int32, (2 * ROWS, 2 * ROWS), 0)
    column = lax.broadcasted_iota(jnp.int32, (2 * ROWS, 2 * ROWS), 1)
    parted = (column == row % 2 * ROWS + row // 2).astype(jnp.float32).astype(jnp.bfloat16)
    copies = []
    results = (
        (mixed_ref, out_gate_ref),
        (grad_out_gate_ref, cot_ref),
        (grad_in_gate_ref, values_ref),
        (grad_values_ref, in_gate_ref),
    )
    for which in range(2):
        lanes = slice(which * ROWS, (which + 1) * ROWS)
        turned = jnp.concatenate(
            [
                ordered_ref[:, part * GROUPS_HERE : (part + 1) * GROUPS_HERE, lanes].reshape(
                    ROWS, ROWS
                )
                for part in range(2)
            ],
            axis=1,
        )
        signal = lax.dot_general(
            parted, turned, (((1,), (1,)), ((), ())), preferred_element_type=jnp.float32
        )
        for slot in (2 * which, 2 * which + 1):
            result_ref, gate_ref = results[slot]
            gate = gate_ref[...].reshape(2 * ROWS, ROWS).astype(jnp.float32)
            results_ref[slot] = (signal * gate).astype(jnp.bfloat16).reshape(ROWS, 2, ROWS)
            copies.append(
                pltpu.make_async_copy(results_ref.at[slot], result_ref, left.at[slot])
            )
            copies[-1].start()
    for second in range(RING):
        total = returned_ref[0, second, :, 2 * ROWS :].astype(jnp.float32)
        for first in range(1, RING):
            total += returned_ref[first, second, :, 2 * ROWS :].astype(jnp.float32)
        total = total * scale
        rows = slice(second * GROUPS_HERE, (second + 1) * GROUPS_HERE)
        sums_ref[rows, :HALF] = total[:GROUPS_HERE]
        sums_ref[rows, HALF:] = total[GROUPS_HERE:]
    copies.append(pltpu.make_async_copy(sums_ref, grad_filter_ref, left.at[len(results)]))
    copies[-1].start()
    for copy in copies:
        copy.wait()


def outcomes(scale, returned, out_gate, in_gate, values_in, out_cotangent):
    whole = pl.BlockSpec(memory_space=pltpu.VMEM)
    signal = jax.ShapeDtypeStruct((ROWS, 2, ROWS), jnp.bfloat16)
    return pl.pallas_call(
        functools.partial(outcome_kernel, scale),
        out_shape=(signal,) * 4
        + (jax.ShapeDtypeStruct((RING * GROUPS_HERE, ROWS), jnp.float32),),
        in_specs=[whole] * 5,
        out_specs=(pl.BlockSpec(memory_space=pl.ANY),) * 5,
        scratch_shapes=[
            pltpu.VMEM((BLOCKS, SIGNALS, 2 * ROWS), jnp.bfloat16),
            pltpu.VMEM((4, ROWS, 2, ROWS), jnp.bfloat16),
            pltpu.VMEM((RING * GROUPS_HERE, ROWS), jnp.float32),
            pltpu.SemaphoreType.DMA((5,)),
        ],
        compiler_params=pltpu.CompilerParams(vmem_limit_bytes=16 * 1024 * 1024),
        cost_estimate=pl.CostEstimate(
            flops=400_000_000, bytes_accessed=3_000_000, transcendentals=0
        ),
        name="outcomes",
    )(returned, out_gate, in_gate, values_in, out_cotangent)


def exchange(value, axis):
    return lax.all_to_all(value, axis, split_axis=0, concat_axis=0, tiled=True)


def local(out_gate, in_gate, values_in, filter_taps, skip_gain, out_cotangent):
    row_count, member_count, group_count = out_gate.shape
    chan_count = lax.axis_size("chan")

    def send_lag(lag):
        pairs = [
            (
                (first * RING + second) * RING + level,
                (first * RING + second) * RING + (level + shift(first, second)) % RING,
            )
            for first in range(RING)
            for second in range(RING)
            for level in range(RING)
        ]
        return lax.ppermute(lag, ("seq", "chan"), pairs)

    outgoing = gated_chunks(out_gate, in_gate, values_in, filter_taps, out_cotangent)
    received = exchange(outgoing.reshape(BLOCKS, SIGNALS, 5 * HALF), "seq")
    returned = exchange(spectral(received, skip_gain, send_lag), "seq")
    norm_factor = 1.0 / math.sqrt(BLOCKS * row_count * member_count * chan_count)
    *gradients, filter_sum = outcomes(
        norm_factor,
        returned.reshape(RING, RING, SIGNALS, 5 * HALF),
        out_gate,
        in_gate,
        values_in,
        out_cotangent,
    )
    return (*gradients, filter_sum.T)


def solution(mesh):
    in_specs = (
        P("seq", "chan", None),
        P("seq", "chan", None),
        P("seq", "chan", None),
        P("seq", None),
        P("chan", None),
        P("seq", "chan", None),
    )
    out_specs = (
        P("seq", "chan", None),
        P("seq", "chan", None),
        P("seq", "chan", None),
        P("seq", "chan", None),
        P("seq", "chan"),
    )
    return jax.shard_map(local, mesh=mesh, in_specs=in_specs, out_specs=out_specs, check_vma=False)
```

```python
import functools
import math

import jax
import jax.numpy as jnp
import ml_dtypes
import numpy as np
from jax import lax
from jax.experimental import pallas as pl
from jax.experimental.pallas import tpu as pltpu
from jax.sharding import PartitionSpec as P

BLOCKS = 64
ROWS = 256
HALF = ROWS // 2
SIGNALS = 8
GROUPS_HERE = 4
KEPT = 64
TILE = 16
FULL = 2 * BLOCKS * ROWS


def split_table(table):
    high = table.astype(ml_dtypes.bfloat16)
    low = (table - high.astype(np.float64)).astype(ml_dtypes.bfloat16)
    return high, low


def tables():
    kept = np.arange(KEPT)[:, None]
    block = np.arange(BLOCKS)[None, :]
    coarse = 2 * math.pi * (((2 * kept + 1) * block) % (4 * BLOCKS)) / (4 * BLOCKS)
    paired = np.stack([np.cos(coarse), -np.sin(coarse)]).reshape(2, -1, TILE, BLOCKS)
    enter_high, enter_low = split_table(paired.swapaxes(0, 1).reshape(2 * KEPT, BLOCKS))
    enter = np.concatenate([enter_high, enter_low], axis=1)
    leave_high, leave_low = split_table(
        np.concatenate([np.cos(coarse.T), -np.sin(coarse.T)], axis=1) * (2.0 / FULL)
    )
    leave = np.concatenate(
        [
            np.concatenate([leave_high, leave_high], axis=1),
            np.concatenate([leave_low, np.zeros_like(leave_low)], axis=1),
        ]
    )
    row = np.arange(ROWS)[None, :]
    twist = 2 * math.pi * (kept + 0.5) * row / FULL
    turn_cos = np.cos(twist).astype(np.float32)
    turn_sin = np.sin(twist).astype(np.float32)
    fine = []
    for odd in (0, 1):
        angle = (
            2
            * math.pi
            * ((np.arange(HALF)[:, None] * (2 * np.arange(HALF)[None, :] + odd)) % ROWS)
            / ROWS
        )
        cos, sin = np.cos(angle), np.sin(angle)
        forth = np.concatenate(
            [np.concatenate([cos, -sin], axis=1), np.concatenate([sin, cos], axis=1)], axis=0
        )
        fine.append((split_table(forth), split_table(forth.T)))
    forth, back = (
        np.stack([np.concatenate([high, low, high]) for high, low in (pair[way] for pair in fine)])
        for way in (0, 1)
    )
    return enter, leave, turn_cos, turn_sin, forth, back


def mxu(left, right):
    return jnp.dot(left, right, preferred_element_type=jnp.float32)


def halves(value):
    high = value.astype(jnp.bfloat16)
    low = (value - high.astype(jnp.float32)).astype(jnp.bfloat16)
    return high, low


class Stages:
    def __init__(self, cos_ref, sin_ref, enter_ref, leave_ref, forth_ref, back_ref):
        self.cos_ref = cos_ref
        self.sin_ref = sin_ref
        self.enter_ref = enter_ref
        self.leave_ref = leave_ref
        self.forth_ref = forth_ref
        self.back_ref = back_ref

    def put(self, pair, odd, rows, real, imag):
        for part, value in enumerate((real, imag)):
            lanes = slice(part * HALF, (part + 1) * HALF)
            for ref, piece in zip(pair, halves(value)):
                ref[odd, rows, lanes] = piece

    def both(self, pair, matrix_ref, odd, rows):
        high = pair[0][odd, rows, :]
        return mxu(jnp.concatenate([pair[1][odd, rows, :], high, high], axis=1), matrix_ref[odd])

    def turns(self, tile):
        return self.cos_ref[tile : tile + TILE, :], self.sin_ref[tile : tile + TILE, :]

    def enter(self, taken, pair, start):
        first = mxu(self.enter_ref[...], jnp.concatenate([taken, taken], axis=0))
        for tile in range(0, KEPT, TILE):
            real = first[2 * tile : 2 * tile + TILE]
            imag = first[2 * tile + TILE : 2 * tile + 2 * TILE]
            turn_cos, turn_sin = self.turns(tile)
            turned_real = real * turn_cos + imag * turn_sin
            turned_imag = imag * turn_cos - real * turn_sin
            rows = slice(start + tile, start + tile + TILE)
            near_real, far_real = turned_real[:, :HALF], turned_real[:, HALF:]
            near_imag, far_imag = turned_imag[:, :HALF], turned_imag[:, HALF:]
            self.put(pair, 0, rows, near_real + far_real, near_imag + far_imag)
            self.put(pair, 1, rows, near_real - far_real, near_imag - far_imag)

    def forth(self, pair, spec_ref, rows):
        for odd in (0, 1):
            spec_ref[odd, rows, :] = self.both(pair, self.forth_ref, odd, rows)

    def back(self, pair, turn_ref, rows):
        for odd in (0, 1):
            turn_ref[odd, rows, :] = self.both(pair, self.back_ref, odd, rows)

    def leave(self, turn_ref, start):
        pieces = [[], [], [], []]
        for tile in range(0, KEPT, TILE):
            rows = slice(start + tile, start + tile + TILE)
            turn_cos, turn_sin = self.turns(tile)
            even, odd = turn_ref[0, rows, :], turn_ref[1, rows, :]
            near, far = even + odd, even - odd
            real = jnp.concatenate([near[:, :HALF], far[:, :HALF]], axis=1)
            imag = jnp.concatenate([near[:, HALF:], far[:, HALF:]], axis=1)
            real_high, real_low = halves(real * turn_cos - imag * turn_sin)
            imag_high, imag_low = halves(imag * turn_cos + real * turn_sin)
            for kept, piece in zip(pieces, (real_high, imag_high, real_low, imag_low)):
                kept.append(piece)
        result = mxu(self.leave_ref[...], jnp.concatenate(sum(pieces, []), axis=0))
        return result[:BLOCKS] + result[BLOCKS:]


MEMBERS = SIGNALS // GROUPS_HERE
PAIRS = 2 * MEMBERS
GROUP_ROWS = PAIRS * KEPT


def every(row):
    return pl.ds(row, BLOCKS, stride=SIGNALS)


def spread(wide_ref, lane, received):
    wide_ref[lane] = received.astype(jnp.float32).reshape(BLOCKS * SIGNALS, HALF)


def gather(wide_ref, lane):
    return wide_ref[lane].reshape(BLOCKS, SIGNALS, HALF).astype(jnp.bfloat16)


def places(group, item):
    which, member = divmod(item, MEMBERS)
    row = member * GROUPS_HERE + group
    return ((2 * which, row), (2 * which + 1, row))


def spot(group, item, offset=0, size=KEPT):
    start = (group * PAIRS + item) * KEPT + offset
    return slice(start, start + size)


def lag_kernel(
    recv_ref,
    enter_ref,
    leave_ref,
    cos_ref,
    sin_ref,
    forth_ref,
    back_ref,
    lag_ref,
    spec_ref,
    wide_ref,
    high_ref,
    low_ref,
    high_lag_ref,
    low_lag_ref,
    turn_ref,
    wide_lag_ref,
):
    stages = Stages(cos_ref, sin_ref, enter_ref, leave_ref, forth_ref, back_ref)
    pair, joined = (high_ref, low_ref), (high_lag_ref, low_lag_ref)
    for lane in range(4):
        spread(wide_ref, lane, recv_ref[:, :, lane * HALF : (lane + 1) * HALF])
    def enter(group):
        for item in range(PAIRS):
            taken = jnp.concatenate(
                [wide_ref[lane, every(row), :] for lane, row in places(group, item)], axis=1
            ).astype(jnp.bfloat16)
            stages.enter(taken, pair, spot(group, item).start)

    enter(0)
    for group in range(GROUPS_HERE):
        if group + 1 < GROUPS_HERE:
            enter(group + 1)
        stages.forth(pair, spec_ref, slice(group * GROUP_ROWS, (group + 1) * GROUP_ROWS))
    for group in range(GROUPS_HERE):
        for odd in (0, 1):
            for tile in range(0, KEPT, TILE):
                real = imag = None
                for member in range(MEMBERS):
                    rows = spot(group, member, tile, TILE)
                    in_real, in_imag = spec_ref[odd, rows, :HALF], spec_ref[odd, rows, HALF:]
                    rows = spot(group, MEMBERS + member, tile, TILE)
                    cot_real, cot_imag = spec_ref[odd, rows, :HALF], spec_ref[odd, rows, HALF:]
                    more_real = cot_real * in_real + cot_imag * in_imag
                    more_imag = cot_imag * in_real - cot_real * in_imag
                    real = more_real if member == 0 else real + more_real
                    imag = more_imag if member == 0 else imag + more_imag
                start = group * KEPT + tile
                stages.put(joined, odd, slice(start, start + TILE), real, imag)
    for half in range(2):
        stages.back(joined, turn_ref, slice(half * 2 * KEPT, (half + 1) * 2 * KEPT))
    for group in range(GROUPS_HERE):
        result = stages.leave(turn_ref, group * KEPT)
        wide_lag_ref[0, every(group), :] = result[:, :HALF]
        wide_lag_ref[0, every(group + GROUPS_HERE), :] = result[:, HALF:]
    lag_ref[...] = gather(wide_lag_ref, 0)


def signal_kernel(
    skip_ref,
    recv_ref,
    spec_ref,
    wide_ref,
    enter_ref,
    leave_ref,
    cos_ref,
    sin_ref,
    forth_ref,
    back_ref,
    send_ref,
    wide_taps_ref,
    high_taps_ref,
    low_taps_ref,
    spec_taps_ref,
    high_ref,
    low_ref,
    turn_ref,
    wide_out_ref,
):
    stages = Stages(cos_ref, sin_ref, enter_ref, leave_ref, forth_ref, back_ref)
    taps_pair, pair = (high_taps_ref, low_taps_ref), (high_ref, low_ref)
    skip = jnp.concatenate([skip_ref[...], jnp.zeros((6, ROWS), jnp.float32)], axis=0)
    gains = pltpu.roll(skip, lax.rem(ROWS - position()[1] * GROUPS_HERE, ROWS), 1)
    spread(wide_taps_ref, 0, recv_ref[:, :, 4 * HALF :])
    for group in range(GROUPS_HERE):
        taken = jnp.concatenate(
            [
                wide_taps_ref[0, every(group), :],
                wide_taps_ref[0, every(group + GROUPS_HERE), :],
            ],
            axis=1,
        ).astype(jnp.bfloat16)
        stages.enter(taken, taps_pair, group * KEPT)
    size = GROUPS_HERE * KEPT // 2
    for part in range(2):
        stages.forth(taps_pair, spec_taps_ref, slice(part * size, (part + 1) * size))

    def multiply(group):
        for odd in (0, 1):
            for tile in range(0, KEPT, TILE):
                rows = slice(group * KEPT + tile, group * KEPT + tile + TILE)
                tap_real, tap_imag = spec_taps_ref[odd, rows, :HALF], spec_taps_ref[odd, rows, HALF:]
                for item in range(PAIRS):
                    rows = spot(group, item, tile, TILE)
                    real, imag = spec_ref[odd, rows, :HALF], spec_ref[odd, rows, HALF:]
                    turn = tap_imag if item < MEMBERS else -tap_imag
                    stages.put(
                        pair,
                        odd,
                        rows,
                        real * tap_real - imag * turn,
                        real * turn + imag * tap_real,
                    )

    def back(group):
        size = GROUP_ROWS // 1
        for part in range(1):
            start = group * GROUP_ROWS + part * size
            stages.back(pair, turn_ref, slice(start, start + size))

    def leave(group):
        for item in range(PAIRS):
            result = stages.leave(turn_ref, spot(group, item).start)
            member = item % MEMBERS
            gain = gains[member : member + 1, group : group + 1]
            for part, (lane, row) in enumerate(places(group, item)):
                direct = wide_ref[lane, every(row), :] * gain
                wide_out_ref[lane, every(row), :] = (
                    result[:, part * HALF : (part + 1) * HALF] + direct
                )

    for stage in (multiply, back, leave):
        for group in range(GROUPS_HERE):
            stage(group)
    for lane in range(4):
        send_ref[:, :, lane * HALF : (lane + 1) * HALF] = gather(wide_out_ref, lane)


def spectral(received, skip_gain, send_lag):
    constants = [jnp.asarray(table) for table in tables()]
    signal_rows, group_rows = GROUPS_HERE * GROUP_ROWS, GROUPS_HERE * KEPT
    whole = pl.BlockSpec(memory_space=pltpu.VMEM)
    params = pltpu.CompilerParams(vmem_limit_bytes=24 * 1024 * 1024)
    lag, spec, wide = pl.pallas_call(
        lag_kernel,
        out_shape=(
            jax.ShapeDtypeStruct((BLOCKS, SIGNALS, HALF), jnp.bfloat16),
            jax.ShapeDtypeStruct((2, signal_rows, ROWS), jnp.float32),
            jax.ShapeDtypeStruct((4, BLOCKS * SIGNALS, HALF), jnp.float32),
        ),
        in_specs=[whole] * 7,
        out_specs=(whole,) * 3,
        scratch_shapes=[
            pltpu.VMEM((2, signal_rows, ROWS), jnp.bfloat16),
            pltpu.VMEM((2, signal_rows, ROWS), jnp.bfloat16),
            pltpu.VMEM((2, group_rows, ROWS), jnp.bfloat16),
            pltpu.VMEM((2, group_rows, ROWS), jnp.bfloat16),
            pltpu.VMEM((2, group_rows, ROWS), jnp.float32),
            pltpu.VMEM((1, BLOCKS * SIGNALS, HALF), jnp.float32),
        ],
        compiler_params=params,
        cost_estimate=pl.CostEstimate(
            flops=3_000_000_000, bytes_accessed=5_000_000, transcendentals=0
        ),
        name="lags",
    )(received, *constants)
    moved = send_lag(lag)
    signals = pl.pallas_call(
        signal_kernel,
        out_shape=jax.ShapeDtypeStruct((BLOCKS, SIGNALS, 4 * HALF), jnp.bfloat16),
        in_specs=[whole] * 10,
        out_specs=whole,
        scratch_shapes=[
            pltpu.VMEM((1, BLOCKS * SIGNALS, HALF), jnp.float32),
            pltpu.VMEM((2, group_rows, ROWS), jnp.bfloat16),
            pltpu.VMEM((2, group_rows, ROWS), jnp.bfloat16),
            pltpu.VMEM((2, group_rows, ROWS), jnp.float32),
            pltpu.VMEM((2, signal_rows, ROWS), jnp.bfloat16),
            pltpu.VMEM((2, signal_rows, ROWS), jnp.bfloat16),
            pltpu.VMEM((2, signal_rows, ROWS), jnp.float32),
            pltpu.VMEM((4, BLOCKS * SIGNALS, HALF), jnp.float32),
        ],
        compiler_params=params,
        cost_estimate=pl.CostEstimate(
            flops=3_000_000_000, bytes_accessed=5_000_000, transcendentals=0
        ),
        name="signals",
    )(skip_gain, received, spec, wide, *constants)
    return jnp.concatenate([signals, moved], axis=2)


RING = 8


def shift(row, column):
    return (row + RING // 2 * (column % 2)) % RING


def position():
    seat, plane = lax.axis_index("seq"), lax.axis_index("chan")
    row, column = lax.div(seat, RING), lax.rem(seat, RING)
    held = lax.rem(plane + row + RING // 2 * lax.rem(column, 2), RING) * RING + column
    return plane, held


def holders(plane):
    return [
        [lax.rem(first - RING // 2 * odd + 2 * RING - plane, RING) for odd in (0, 1)]
        for first in range(RING)
    ]


def gate_kernel(
    out_gate_ref,
    in_gate_ref,
    values_ref,
    taps_ref,
    cot_ref,
    send_ref,
    gates_ref,
    held_taps_ref,
    arrived,
):
    sources = (in_gate_ref, values_ref, cot_ref, out_gate_ref)
    copies = [
        pltpu.make_async_copy(source, gates_ref.at[slot], arrived.at[slot])
        for slot, source in enumerate(sources)
    ]
    copies.append(pltpu.make_async_copy(taps_ref, held_taps_ref, arrived.at[len(sources)]))
    for copy in copies:
        copy.start()

    row = lax.broadcasted_iota(jnp.int32, (2 * ROWS, 2 * ROWS), 0)
    column = lax.broadcasted_iota(jnp.int32, (2 * ROWS, 2 * ROWS), 1)
    parted = (row == column % ROWS * 2 + column // ROWS).astype(jnp.float32)
    parted = parted.astype(jnp.bfloat16)
    plain = (row == column)[:ROWS, :ROWS].astype(jnp.float32).astype(jnp.bfloat16)

    def turned(value, order):
        return lax.dot_general(
            value, order, (((0,), (0,)), ((), ())), preferred_element_type=jnp.float32
        ).astype(jnp.bfloat16)

    owners = holders(position()[0])

    def send(part, lanes, value):
        rows = slice(part * GROUPS_HERE, (part + 1) * GROUPS_HERE)
        value = value.reshape(BLOCKS, GROUPS_HERE, -1)
        for first in range(RING):
            for second in range(RING):
                send_ref[owners[first][second % 2], second, rows, lanes] = value[
                    first * RING + second
                ]

    for which in range(2):
        left, right = 2 * which, 2 * which + 1
        copies[left].wait()
        copies[right].wait()
        product = gates_ref[left].reshape(2 * ROWS, ROWS).astype(jnp.float32) * gates_ref[
            right
        ].reshape(2 * ROWS, ROWS).astype(jnp.float32)
        signal = turned(product.astype(jnp.bfloat16), parted)
        for member in range(2):
            send(
                member,
                slice(which * ROWS, (which + 1) * ROWS),
                signal[:, member * ROWS : (member + 1) * ROWS],
            )
    copies[-1].wait()
    taps = turned(held_taps_ref[...], plain)
    for half in range(2):
        send(half, slice(2 * ROWS, None), taps[:, half * HALF : (half + 1) * HALF])


def gated_chunks(out_gate, in_gate, values_in, filter_taps, out_cotangent):
    return pl.pallas_call(
        gate_kernel,
        out_shape=jax.ShapeDtypeStruct((RING, RING, SIGNALS, 5 * HALF), jnp.bfloat16),
        in_specs=[pl.BlockSpec(memory_space=pltpu.HBM)] * 5,
        out_specs=pl.BlockSpec(memory_space=pltpu.VMEM),
        scratch_shapes=[
            pltpu.VMEM((4, ROWS, 2, ROWS), jnp.bfloat16),
            pltpu.VMEM((ROWS, ROWS), jnp.bfloat16),
            pltpu.SemaphoreType.DMA((5,)),
        ],
        compiler_params=pltpu.CompilerParams(vmem_limit_bytes=16 * 1024 * 1024),
        cost_estimate=pl.CostEstimate(
            flops=400_000_000, bytes_accessed=2_000_000, transcendentals=0
        ),
        name="gates",
    )(
        *(
            pltpu.with_memory_space_constraint(value, pltpu.HBM)
            for value in (out_gate, in_gate, values_in, filter_taps, out_cotangent)
        )
    )


def outcome_kernel(
    scale,
    returned_ref,
    out_gate_ref,
    in_gate_ref,
    values_ref,
    cot_ref,
    mixed_ref,
    grad_out_gate_ref,
    grad_in_gate_ref,
    grad_values_ref,
    grad_filter_ref,
    ordered_ref,
    results_ref,
    sums_ref,
    left,
):
    owners = holders(position()[0])
    for first in range(RING):
        for second in range(RING):
            ordered_ref[first * RING + second] = returned_ref[
                owners[first][second % 2], second, :, : 2 * ROWS
            ]
    row = lax.broadcasted_iota(jnp.int32, (2 * ROWS, 2 * ROWS), 0)
    column = lax.broadcasted_iota(jnp.int32, (2 * ROWS, 2 * ROWS), 1)
    parted = (column == row % 2 * ROWS + row // 2).astype(jnp.float32).astype(jnp.bfloat16)
    copies = []
    results = (
        (mixed_ref, out_gate_ref),
        (grad_out_gate_ref, cot_ref),
        (grad_in_gate_ref, values_ref),
        (grad_values_ref, in_gate_ref),
    )
    for which in range(2):
        lanes = slice(which * ROWS, (which + 1) * ROWS)
        turned = jnp.concatenate(
            [
                ordered_ref[:, part * GROUPS_HERE : (part + 1) * GROUPS_HERE, lanes].reshape(
                    ROWS, ROWS
                )
                for part in range(2)
            ],
            axis=1,
        )
        signal = lax.dot_general(
            parted, turned, (((1,), (1,)), ((), ())), preferred_element_type=jnp.float32
        )
        for slot in (2 * which, 2 * which + 1):
            result_ref, gate_ref = results[slot]
            gate = gate_ref[...].reshape(2 * ROWS, ROWS).astype(jnp.float32)
            results_ref[slot] = (signal * gate).astype(jnp.bfloat16).reshape(ROWS, 2, ROWS)
            copies.append(
                pltpu.make_async_copy(results_ref.at[slot], result_ref, left.at[slot])
            )
            copies[-1].start()
    for second in range(RING):
        total = returned_ref[0, second, :, 2 * ROWS :].astype(jnp.float32)
        for first in range(1, RING):
            total += returned_ref[first, second, :, 2 * ROWS :].astype(jnp.float32)
        total = total * scale
        rows = slice(second * GROUPS_HERE, (second + 1) * GROUPS_HERE)
        sums_ref[rows, :HALF] = total[:GROUPS_HERE]
        sums_ref[rows, HALF:] = total[GROUPS_HERE:]
    copies.append(pltpu.make_async_copy(sums_ref, grad_filter_ref, left.at[len(results)]))
    copies[-1].start()
    for copy in copies:
        copy.wait()


def outcomes(scale, returned, out_gate, in_gate, values_in, out_cotangent):
    whole = pl.BlockSpec(memory_space=pltpu.VMEM)
    signal = jax.ShapeDtypeStruct((ROWS, 2, ROWS), jnp.bfloat16)
    return pl.pallas_call(
        functools.partial(outcome_kernel, scale),
        out_shape=(signal,) * 4
        + (jax.ShapeDtypeStruct((RING * GROUPS_HERE, ROWS), jnp.float32),),
        in_specs=[whole] * 5,
        out_specs=(pl.BlockSpec(memory_space=pl.ANY),) * 5,
        scratch_shapes=[
            pltpu.VMEM((BLOCKS, SIGNALS, 2 * ROWS), jnp.bfloat16),
            pltpu.VMEM((4, ROWS, 2, ROWS), jnp.bfloat16),
            pltpu.VMEM((RING * GROUPS_HERE, ROWS), jnp.float32),
            pltpu.SemaphoreType.DMA((5,)),
        ],
        compiler_params=pltpu.CompilerParams(vmem_limit_bytes=16 * 1024 * 1024),
        cost_estimate=pl.CostEstimate(
            flops=400_000_000, bytes_accessed=3_000_000, transcendentals=0
        ),
        name="outcomes",
    )(returned, out_gate, in_gate, values_in, out_cotangent)


def exchange(value, axis):
    return lax.all_to_all(value, axis, split_axis=0, concat_axis=0, tiled=True)


def local(out_gate, in_gate, values_in, filter_taps, skip_gain, out_cotangent):
    row_count, member_count, group_count = out_gate.shape
    chan_count = lax.axis_size("chan")

    def send_lag(lag):
        pairs = [
            (
                (first * RING + second) * RING + level,
                (first * RING + second) * RING + (level + shift(first, second)) % RING,
            )
            for first in range(RING)
            for second in range(RING)
            for level in range(RING)
        ]
        return lax.ppermute(lag, ("seq", "chan"), pairs)

    outgoing = gated_chunks(out_gate, in_gate, values_in, filter_taps, out_cotangent)
    received = exchange(outgoing.reshape(BLOCKS, SIGNALS, 5 * HALF), "seq")
    returned = exchange(spectral(received, skip_gain, send_lag), "seq")
    norm_factor = 1.0 / math.sqrt(BLOCKS * row_count * member_count * chan_count)
    *gradients, filter_sum = outcomes(
        norm_factor,
        returned.reshape(RING, RING, SIGNALS, 5 * HALF),
        out_gate,
        in_gate,
        values_in,
        out_cotangent,
    )
    return (*gradients, filter_sum.T)


def solution(mesh):
    in_specs = (
        P("seq", "chan", None),
        P("seq", "chan", None),
        P("seq", "chan", None),
        P("seq", None),
        P("chan", None),
        P("seq", "chan", None),
    )
    out_specs = (
        P("seq", "chan", None),
        P("seq", "chan", None),
        P("seq", "chan", None),
        P("seq", "chan", None),
        P("seq", "chan"),
    )
    return jax.shard_map(local, mesh=mesh, in_specs=in_specs, out_specs=out_specs, check_vma=False)
```

```python
import functools
import math

import jax
import jax.numpy as jnp
import ml_dtypes
import numpy as np
from jax import lax
from jax.experimental import pallas as pl
from jax.experimental.pallas import tpu as pltpu
from jax.sharding import PartitionSpec as P

BLOCKS = 64
ROWS = 256
HALF = ROWS // 2
SIGNALS = 8
GROUPS_HERE = 4
KEPT = 64
TILE = 16
FULL = 2 * BLOCKS * ROWS


def split_table(table):
    high = table.astype(ml_dtypes.bfloat16)
    low = (table - high.astype(np.float64)).astype(ml_dtypes.bfloat16)
    return high, low


def tables():
    kept = np.arange(KEPT)[:, None]
    block = np.arange(BLOCKS)[None, :]
    coarse = 2 * math.pi * (((2 * kept + 1) * block) % (4 * BLOCKS)) / (4 * BLOCKS)
    paired = np.stack([np.cos(coarse), -np.sin(coarse)]).reshape(2, -1, TILE, BLOCKS)
    enter_high, enter_low = split_table(paired.swapaxes(0, 1).reshape(2 * KEPT, BLOCKS))
    enter = np.concatenate([enter_high, enter_low], axis=1)
    leave_high, leave_low = split_table(
        np.concatenate([np.cos(coarse.T), -np.sin(coarse.T)], axis=1) * (2.0 / FULL)
    )
    leave = np.concatenate(
        [
            np.concatenate([leave_high, leave_high], axis=1),
            np.concatenate([leave_low, np.zeros_like(leave_low)], axis=1),
        ]
    )
    row = np.arange(ROWS)[None, :]
    twist = 2 * math.pi * (kept + 0.5) * row / FULL
    turn_cos = np.cos(twist).astype(np.float32)
    turn_sin = np.sin(twist).astype(np.float32)
    fine = []
    for odd in (0, 1):
        angle = (
            2
            * math.pi
            * ((np.arange(HALF)[:, None] * (2 * np.arange(HALF)[None, :] + odd)) % ROWS)
            / ROWS
        )
        cos, sin = np.cos(angle), np.sin(angle)
        forth = np.concatenate(
            [np.concatenate([cos, -sin], axis=1), np.concatenate([sin, cos], axis=1)], axis=0
        )
        fine.append((split_table(forth), split_table(forth.T)))
    forth, back = (
        np.stack([np.concatenate([high, low, high]) for high, low in (pair[way] for pair in fine)])
        for way in (0, 1)
    )
    return enter, leave, turn_cos, turn_sin, forth, back


def mxu(left, right):
    return jnp.dot(left, right, preferred_element_type=jnp.float32)


def halves(value):
    high = value.astype(jnp.bfloat16)
    low = (value - high.astype(jnp.float32)).astype(jnp.bfloat16)
    return high, low


class Stages:
    def __init__(self, cos_ref, sin_ref, enter_ref, leave_ref, forth_ref, back_ref):
        self.cos_ref = cos_ref
        self.sin_ref = sin_ref
        self.enter_ref = enter_ref
        self.leave_ref = leave_ref
        self.forth_ref = forth_ref
        self.back_ref = back_ref

    def put(self, pair, odd, rows, real, imag):
        for part, value in enumerate((real, imag)):
            lanes = slice(part * HALF, (part + 1) * HALF)
            for ref, piece in zip(pair, halves(value)):
                ref[odd, rows, lanes] = piece

    def both(self, pair, matrix_ref, odd, rows):
        high = pair[0][odd, rows, :]
        return mxu(jnp.concatenate([pair[1][odd, rows, :], high, high], axis=1), matrix_ref[odd])

    def turns(self, tile):
        return self.cos_ref[tile : tile + TILE, :], self.sin_ref[tile : tile + TILE, :]

    def enter(self, taken, pair, start):
        first = mxu(self.enter_ref[...], jnp.concatenate([taken, taken], axis=0))
        for tile in range(0, KEPT, TILE):
            real = first[2 * tile : 2 * tile + TILE]
            imag = first[2 * tile + TILE : 2 * tile + 2 * TILE]
            turn_cos, turn_sin = self.turns(tile)
            turned_real = real * turn_cos + imag * turn_sin
            turned_imag = imag * turn_cos - real * turn_sin
            rows = slice(start + tile, start + tile + TILE)
            near_real, far_real = turned_real[:, :HALF], turned_real[:, HALF:]
            near_imag, far_imag = turned_imag[:, :HALF], turned_imag[:, HALF:]
            self.put(pair, 0, rows, near_real + far_real, near_imag + far_imag)
            self.put(pair, 1, rows, near_real - far_real, near_imag - far_imag)

    def forth(self, pair, spec_ref, rows):
        for odd in (0, 1):
            spec_ref[odd, rows, :] = self.both(pair, self.forth_ref, odd, rows)

    def back(self, pair, turn_ref, rows):
        for odd in (0, 1):
            turn_ref[odd, rows, :] = self.both(pair, self.back_ref, odd, rows)

    def leave(self, turn_ref, start):
        pieces = [[], [], [], []]
        for tile in range(0, KEPT, TILE):
            rows = slice(start + tile, start + tile + TILE)
            turn_cos, turn_sin = self.turns(tile)
            even, odd = turn_ref[0, rows, :], turn_ref[1, rows, :]
            near, far = even + odd, even - odd
            real = jnp.concatenate([near[:, :HALF], far[:, :HALF]], axis=1)
            imag = jnp.concatenate([near[:, HALF:], far[:, HALF:]], axis=1)
            real_high, real_low = halves(real * turn_cos - imag * turn_sin)
            imag_high, imag_low = halves(imag * turn_cos + real * turn_sin)
            for kept, piece in zip(pieces, (real_high, imag_high, real_low, imag_low)):
                kept.append(piece)
        result = mxu(self.leave_ref[...], jnp.concatenate(sum(pieces, []), axis=0))
        return result[:BLOCKS] + result[BLOCKS:]


MEMBERS = SIGNALS // GROUPS_HERE
PAIRS = 2 * MEMBERS
GROUP_ROWS = PAIRS * KEPT


def every(row):
    return pl.ds(row, BLOCKS, stride=SIGNALS)


def spread(wide_ref, lane, received):
    wide_ref[lane] = received.astype(jnp.float32).reshape(BLOCKS * SIGNALS, HALF)


def gather(wide_ref, lane):
    return wide_ref[lane].reshape(BLOCKS, SIGNALS, HALF).astype(jnp.bfloat16)


def places(group, item):
    which, member = divmod(item, MEMBERS)
    row = member * GROUPS_HERE + group
    return ((2 * which, row), (2 * which + 1, row))


def spot(group, item, offset=0, size=KEPT):
    start = (group * PAIRS + item) * KEPT + offset
    return slice(start, start + size)


def lag_kernel(
    recv_ref,
    enter_ref,
    leave_ref,
    cos_ref,
    sin_ref,
    forth_ref,
    back_ref,
    lag_ref,
    spec_ref,
    wide_ref,
    high_ref,
    low_ref,
    high_lag_ref,
    low_lag_ref,
    turn_ref,
    wide_lag_ref,
):
    stages = Stages(cos_ref, sin_ref, enter_ref, leave_ref, forth_ref, back_ref)
    pair, joined = (high_ref, low_ref), (high_lag_ref, low_lag_ref)
    for lane in range(4):
        spread(wide_ref, lane, recv_ref[:, :, lane * HALF : (lane + 1) * HALF])
    def enter(group):
        for item in range(PAIRS):
            taken = jnp.concatenate(
                [wide_ref[lane, every(row), :] for lane, row in places(group, item)], axis=1
            ).astype(jnp.bfloat16)
            stages.enter(taken, pair, spot(group, item).start)

    enter(0)
    for group in range(GROUPS_HERE):
        if group + 1 < GROUPS_HERE:
            enter(group + 1)
        stages.forth(pair, spec_ref, slice(group * GROUP_ROWS, (group + 1) * GROUP_ROWS))
    for group in range(GROUPS_HERE):
        for odd in (0, 1):
            for tile in range(0, KEPT, TILE):
                real = imag = None
                for member in range(MEMBERS):
                    rows = spot(group, member, tile, TILE)
                    in_real, in_imag = spec_ref[odd, rows, :HALF], spec_ref[odd, rows, HALF:]
                    rows = spot(group, MEMBERS + member, tile, TILE)
                    cot_real, cot_imag = spec_ref[odd, rows, :HALF], spec_ref[odd, rows, HALF:]
                    more_real = cot_real * in_real + cot_imag * in_imag
                    more_imag = cot_imag * in_real - cot_real * in_imag
                    real = more_real if member == 0 else real + more_real
                    imag = more_imag if member == 0 else imag + more_imag
                start = group * KEPT + tile
                stages.put(joined, odd, slice(start, start + TILE), real, imag)
    for half in range(2):
        stages.back(joined, turn_ref, slice(half * 2 * KEPT, (half + 1) * 2 * KEPT))
    for group in range(GROUPS_HERE):
        result = stages.leave(turn_ref, group * KEPT)
        wide_lag_ref[0, every(group), :] = result[:, :HALF]
        wide_lag_ref[0, every(group + GROUPS_HERE), :] = result[:, HALF:]
    lag_ref[...] = gather(wide_lag_ref, 0)


def signal_kernel(
    skip_ref,
    recv_ref,
    spec_ref,
    wide_ref,
    enter_ref,
    leave_ref,
    cos_ref,
    sin_ref,
    forth_ref,
    back_ref,
    send_ref,
    wide_taps_ref,
    high_taps_ref,
    low_taps_ref,
    spec_taps_ref,
    high_ref,
    low_ref,
    turn_ref,
    wide_out_ref,
):
    stages = Stages(cos_ref, sin_ref, enter_ref, leave_ref, forth_ref, back_ref)
    taps_pair, pair = (high_taps_ref, low_taps_ref), (high_ref, low_ref)
    skip = jnp.concatenate([skip_ref[...], jnp.zeros((6, ROWS), jnp.float32)], axis=0)
    gains = pltpu.roll(skip, lax.rem(ROWS - position()[1] * GROUPS_HERE, ROWS), 1)
    spread(wide_taps_ref, 0, recv_ref[:, :, 4 * HALF :])
    for group in range(GROUPS_HERE):
        taken = jnp.concatenate(
            [
                wide_taps_ref[0, every(group), :],
                wide_taps_ref[0, every(group + GROUPS_HERE), :],
            ],
            axis=1,
        ).astype(jnp.bfloat16)
        stages.enter(taken, taps_pair, group * KEPT)
    size = GROUPS_HERE * KEPT // 2
    for part in range(2):
        stages.forth(taps_pair, spec_taps_ref, slice(part * size, (part + 1) * size))

    def multiply(group):
        for odd in (0, 1):
            for tile in range(0, KEPT, TILE):
                rows = slice(group * KEPT + tile, group * KEPT + tile + TILE)
                tap_real, tap_imag = spec_taps_ref[odd, rows, :HALF], spec_taps_ref[odd, rows, HALF:]
                for item in range(PAIRS):
                    rows = spot(group, item, tile, TILE)
                    real, imag = spec_ref[odd, rows, :HALF], spec_ref[odd, rows, HALF:]
                    turn = tap_imag if item < MEMBERS else -tap_imag
                    stages.put(
                        pair,
                        odd,
                        rows,
                        real * tap_real - imag * turn,
                        real * turn + imag * tap_real,
                    )

    def back(group):
        size = GROUP_ROWS // 1
        for part in range(1):
            start = group * GROUP_ROWS + part * size
            stages.back(pair, turn_ref, slice(start, start + size))

    def leave(group):
        for item in range(PAIRS):
            result = stages.leave(turn_ref, spot(group, item).start)
            member = item % MEMBERS
            gain = gains[member : member + 1, group : group + 1]
            for part, (lane, row) in enumerate(places(group, item)):
                direct = wide_ref[lane, every(row), :] * gain
                wide_out_ref[lane, every(row), :] = (
                    result[:, part * HALF : (part + 1) * HALF] + direct
                )

    for stage in (multiply, back, leave):
        for group in range(GROUPS_HERE):
            stage(group)
    for lane in range(4):
        send_ref[:, :, lane * HALF : (lane + 1) * HALF] = gather(wide_out_ref, lane)


def spectral(received, skip_gain, send_lag):
    constants = [jnp.asarray(table) for table in tables()]
    signal_rows, group_rows = GROUPS_HERE * GROUP_ROWS, GROUPS_HERE * KEPT
    whole = pl.BlockSpec(memory_space=pltpu.VMEM)
    params = pltpu.CompilerParams(vmem_limit_bytes=24 * 1024 * 1024)
    lag, spec, wide = pl.pallas_call(
        lag_kernel,
        out_shape=(
            jax.ShapeDtypeStruct((BLOCKS, SIGNALS, HALF), jnp.bfloat16),
            jax.ShapeDtypeStruct((2, signal_rows, ROWS), jnp.float32),
            jax.ShapeDtypeStruct((4, BLOCKS * SIGNALS, HALF), jnp.float32),
        ),
        in_specs=[whole] * 7,
        out_specs=(whole,) * 3,
        scratch_shapes=[
            pltpu.VMEM((2, signal_rows, ROWS), jnp.bfloat16),
            pltpu.VMEM((2, signal_rows, ROWS), jnp.bfloat16),
            pltpu.VMEM((2, group_rows, ROWS), jnp.bfloat16),
            pltpu.VMEM((2, group_rows, ROWS), jnp.bfloat16),
            pltpu.VMEM((2, group_rows, ROWS), jnp.float32),
            pltpu.VMEM((1, BLOCKS * SIGNALS, HALF), jnp.float32),
        ],
        compiler_params=params,
        cost_estimate=pl.CostEstimate(
            flops=3_000_000_000, bytes_accessed=5_000_000, transcendentals=0
        ),
        name="lags",
    )(received, *constants)
    moved = send_lag(lag)
    signals = pl.pallas_call(
        signal_kernel,
        out_shape=jax.ShapeDtypeStruct((BLOCKS, SIGNALS, 4 * HALF), jnp.bfloat16),
        in_specs=[whole] * 10,
        out_specs=whole,
        scratch_shapes=[
            pltpu.VMEM((1, BLOCKS * SIGNALS, HALF), jnp.float32),
            pltpu.VMEM((2, group_rows, ROWS), jnp.bfloat16),
            pltpu.VMEM((2, group_rows, ROWS), jnp.bfloat16),
            pltpu.VMEM((2, group_rows, ROWS), jnp.float32),
            pltpu.VMEM((2, signal_rows, ROWS), jnp.bfloat16),
            pltpu.VMEM((2, signal_rows, ROWS), jnp.bfloat16),
            pltpu.VMEM((2, signal_rows, ROWS), jnp.float32),
            pltpu.VMEM((4, BLOCKS * SIGNALS, HALF), jnp.float32),
        ],
        compiler_params=params,
        cost_estimate=pl.CostEstimate(
            flops=3_000_000_000, bytes_accessed=5_000_000, transcendentals=0
        ),
        name="signals",
    )(skip_gain, received, spec, wide, *constants)
    return jnp.concatenate([signals, moved], axis=2)


RING = 8


def shift(row, column):
    return (row + RING // 2 * (column % 2)) % RING


def position():
    seat, plane = lax.axis_index("seq"), lax.axis_index("chan")
    row, column = lax.div(seat, RING), lax.rem(seat, RING)
    held = lax.rem(RING - plane + row + RING // 2 * lax.rem(column, 2), RING) * RING + column
    return plane, held


def holders(plane):
    return [
        [lax.rem(first - RING // 2 * odd + RING + plane, RING) for odd in (0, 1)]
        for first in range(RING)
    ]


def gate_kernel(
    out_gate_ref,
    in_gate_ref,
    values_ref,
    taps_ref,
    cot_ref,
    send_ref,
    gates_ref,
    held_taps_ref,
    arrived,
):
    sources = (in_gate_ref, values_ref, cot_ref, out_gate_ref)
    copies = [
        pltpu.make_async_copy(source, gates_ref.at[slot], arrived.at[slot])
        for slot, source in enumerate(sources)
    ]
    copies.append(pltpu.make_async_copy(taps_ref, held_taps_ref, arrived.at[len(sources)]))
    for copy in copies:
        copy.start()

    row = lax.broadcasted_iota(jnp.int32, (2 * ROWS, 2 * ROWS), 0)
    column = lax.broadcasted_iota(jnp.int32, (2 * ROWS, 2 * ROWS), 1)
    parted = (row == column % ROWS * 2 + column // ROWS).astype(jnp.float32)
    parted = parted.astype(jnp.bfloat16)
    plain = (row == column)[:ROWS, :ROWS].astype(jnp.float32).astype(jnp.bfloat16)

    def turned(value, order):
        return lax.dot_general(
            value, order, (((0,), (0,)), ((), ())), preferred_element_type=jnp.float32
        ).astype(jnp.bfloat16)

    owners = holders(position()[0])

    def send(part, lanes, value):
        rows = slice(part * GROUPS_HERE, (part + 1) * GROUPS_HERE)
        value = value.reshape(BLOCKS, GROUPS_HERE, -1)
        for first in range(RING):
            for second in range(RING):
                send_ref[owners[first][second % 2], second, rows, lanes] = value[
                    first * RING + second
                ]

    for which in range(2):
        left, right = 2 * which, 2 * which + 1
        copies[left].wait()
        copies[right].wait()
        product = gates_ref[left].reshape(2 * ROWS, ROWS).astype(jnp.float32) * gates_ref[
            right
        ].reshape(2 * ROWS, ROWS).astype(jnp.float32)
        signal = turned(product.astype(jnp.bfloat16), parted)
        for member in range(2):
            send(
                member,
                slice(which * ROWS, (which + 1) * ROWS),
                signal[:, member * ROWS : (member + 1) * ROWS],
            )
    copies[-1].wait()
    taps = turned(held_taps_ref[...], plain)
    for half in range(2):
        send(half, slice(2 * ROWS, None), taps[:, half * HALF : (half + 1) * HALF])


def gated_chunks(out_gate, in_gate, values_in, filter_taps, out_cotangent):
    return pl.pallas_call(
        gate_kernel,
        out_shape=jax.ShapeDtypeStruct((RING, RING, SIGNALS, 5 * HALF), jnp.bfloat16),
        in_specs=[pl.BlockSpec(memory_space=pltpu.HBM)] * 5,
        out_specs=pl.BlockSpec(memory_space=pltpu.VMEM),
        scratch_shapes=[
            pltpu.VMEM((4, ROWS, 2, ROWS), jnp.bfloat16),
            pltpu.VMEM((ROWS, ROWS), jnp.bfloat16),
            pltpu.SemaphoreType.DMA((5,)),
        ],
        compiler_params=pltpu.CompilerParams(vmem_limit_bytes=16 * 1024 * 1024),
        cost_estimate=pl.CostEstimate(
            flops=400_000_000, bytes_accessed=2_000_000, transcendentals=0
        ),
        name="gates",
    )(
        *(
            pltpu.with_memory_space_constraint(value, pltpu.HBM)
            for value in (out_gate, in_gate, values_in, filter_taps, out_cotangent)
        )
    )


def outcome_kernel(
    scale,
    returned_ref,
    out_gate_ref,
    in_gate_ref,
    values_ref,
    cot_ref,
    mixed_ref,
    grad_out_gate_ref,
    grad_in_gate_ref,
    grad_values_ref,
    grad_filter_ref,
    ordered_ref,
    results_ref,
    sums_ref,
    left,
):
    owners = holders(position()[0])
    for first in range(RING):
        for second in range(RING):
            ordered_ref[first * RING + second] = returned_ref[
                owners[first][second % 2], second, :, : 2 * ROWS
            ]
    row = lax.broadcasted_iota(jnp.int32, (2 * ROWS, 2 * ROWS), 0)
    column = lax.broadcasted_iota(jnp.int32, (2 * ROWS, 2 * ROWS), 1)
    parted = (column == row % 2 * ROWS + row // 2).astype(jnp.float32).astype(jnp.bfloat16)
    copies = []
    results = (
        (mixed_ref, out_gate_ref),
        (grad_out_gate_ref, cot_ref),
        (grad_in_gate_ref, values_ref),
        (grad_values_ref, in_gate_ref),
    )
    for which in range(2):
        lanes = slice(which * ROWS, (which + 1) * ROWS)
        turned = jnp.concatenate(
            [
                ordered_ref[:, part * GROUPS_HERE : (part + 1) * GROUPS_HERE, lanes].reshape(
                    ROWS, ROWS
                )
                for part in range(2)
            ],
            axis=1,
        )
        signal = lax.dot_general(
            parted, turned, (((1,), (1,)), ((), ())), preferred_element_type=jnp.float32
        )
        for slot in (2 * which, 2 * which + 1):
            result_ref, gate_ref = results[slot]
            gate = gate_ref[...].reshape(2 * ROWS, ROWS).astype(jnp.float32)
            results_ref[slot] = (signal * gate).astype(jnp.bfloat16).reshape(ROWS, 2, ROWS)
            copies.append(
                pltpu.make_async_copy(results_ref.at[slot], result_ref, left.at[slot])
            )
            copies[-1].start()
    for second in range(RING):
        total = returned_ref[0, second, :, 2 * ROWS :].astype(jnp.float32)
        for first in range(1, RING):
            total += returned_ref[first, second, :, 2 * ROWS :].astype(jnp.float32)
        total = total * scale
        rows = slice(second * GROUPS_HERE, (second + 1) * GROUPS_HERE)
        sums_ref[rows, :HALF] = total[:GROUPS_HERE]
        sums_ref[rows, HALF:] = total[GROUPS_HERE:]
    copies.append(pltpu.make_async_copy(sums_ref, grad_filter_ref, left.at[len(results)]))
    copies[-1].start()
    for copy in copies:
        copy.wait()


def outcomes(scale, returned, out_gate, in_gate, values_in, out_cotangent):
    whole = pl.BlockSpec(memory_space=pltpu.VMEM)
    signal = jax.ShapeDtypeStruct((ROWS, 2, ROWS), jnp.bfloat16)
    return pl.pallas_call(
        functools.partial(outcome_kernel, scale),
        out_shape=(signal,) * 4
        + (jax.ShapeDtypeStruct((RING * GROUPS_HERE, ROWS), jnp.float32),),
        in_specs=[whole] * 5,
        out_specs=(pl.BlockSpec(memory_space=pl.ANY),) * 5,
        scratch_shapes=[
            pltpu.VMEM((BLOCKS, SIGNALS, 2 * ROWS), jnp.bfloat16),
            pltpu.VMEM((4, ROWS, 2, ROWS), jnp.bfloat16),
            pltpu.VMEM((RING * GROUPS_HERE, ROWS), jnp.float32),
            pltpu.SemaphoreType.DMA((5,)),
        ],
        compiler_params=pltpu.CompilerParams(vmem_limit_bytes=16 * 1024 * 1024),
        cost_estimate=pl.CostEstimate(
            flops=400_000_000, bytes_accessed=3_000_000, transcendentals=0
        ),
        name="outcomes",
    )(returned, out_gate, in_gate, values_in, out_cotangent)


def exchange(value, axis):
    return lax.all_to_all(value, axis, split_axis=0, concat_axis=0, tiled=True)


def local(out_gate, in_gate, values_in, filter_taps, skip_gain, out_cotangent):
    row_count, member_count, group_count = out_gate.shape
    chan_count = lax.axis_size("chan")

    def send_lag(lag):
        pairs = [
            (
                (first * RING + second) * RING + level,
                (first * RING + second) * RING + (shift(first, second) - level) % RING,
            )
            for first in range(RING)
            for second in range(RING)
            for level in range(RING)
        ]
        return lax.ppermute(lag, ("seq", "chan"), pairs)

    outgoing = gated_chunks(out_gate, in_gate, values_in, filter_taps, out_cotangent)
    received = exchange(outgoing.reshape(BLOCKS, SIGNALS, 5 * HALF), "seq")
    returned = exchange(spectral(received, skip_gain, send_lag), "seq")
    norm_factor = 1.0 / math.sqrt(BLOCKS * row_count * member_count * chan_count)
    *gradients, filter_sum = outcomes(
        norm_factor,
        returned.reshape(RING, RING, SIGNALS, 5 * HALF),
        out_gate,
        in_gate,
        values_in,
        out_cotangent,
    )
    return (*gradients, filter_sum.T)


def solution(mesh):
    in_specs = (
        P("seq", "chan", None),
        P("seq", "chan", None),
        P("seq", "chan", None),
        P("seq", None),
        P("chan", None),
        P("seq", "chan", None),
    )
    out_specs = (
        P("seq", "chan", None),
        P("seq", "chan", None),
        P("seq", "chan", None),
        P("seq", "chan", None),
        P("seq", "chan"),
    )
    return jax.shard_map(local, mesh=mesh, in_specs=in_specs, out_specs=out_specs, check_vma=False)
```

```python
import functools
import math

import jax
import jax.numpy as jnp
import ml_dtypes
import numpy as np
from jax import lax
from jax.experimental import pallas as pl
from jax.experimental.pallas import tpu as pltpu
from jax.sharding import PartitionSpec as P

BLOCKS = 64
ROWS = 256
HALF = ROWS // 2
SIGNALS = 8
GROUPS_HERE = 4
KEPT = 64
TILE = 16
FULL = 2 * BLOCKS * ROWS


def split_table(table):
    high = table.astype(ml_dtypes.bfloat16)
    low = (table - high.astype(np.float64)).astype(ml_dtypes.bfloat16)
    return high, low


def tables():
    kept = np.arange(KEPT)[:, None]
    block = np.arange(BLOCKS)[None, :]
    coarse = 2 * math.pi * (((2 * kept + 1) * block) % (4 * BLOCKS)) / (4 * BLOCKS)
    paired = np.stack([np.cos(coarse), -np.sin(coarse)]).reshape(2, -1, TILE, BLOCKS)
    enter_high, enter_low = split_table(paired.swapaxes(0, 1).reshape(2 * KEPT, BLOCKS))
    enter = np.concatenate([enter_high, enter_low], axis=1)
    leave_high, leave_low = split_table(
        np.concatenate([np.cos(coarse.T), -np.sin(coarse.T)], axis=1) * (2.0 / FULL)
    )
    leave = np.concatenate(
        [
            np.concatenate([leave_high, leave_high], axis=1),
            np.concatenate([leave_low, np.zeros_like(leave_low)], axis=1),
        ]
    )
    row = np.arange(ROWS)[None, :]
    twist = 2 * math.pi * (kept + 0.5) * row / FULL
    turn_cos = np.cos(twist).astype(np.float32)
    turn_sin = np.sin(twist).astype(np.float32)
    fine = []
    for odd in (0, 1):
        angle = (
            2
            * math.pi
            * ((np.arange(HALF)[:, None] * (2 * np.arange(HALF)[None, :] + odd)) % ROWS)
            / ROWS
        )
        cos, sin = np.cos(angle), np.sin(angle)
        forth = np.concatenate(
            [np.concatenate([cos, -sin], axis=1), np.concatenate([sin, cos], axis=1)], axis=0
        )
        fine.append((split_table(forth), split_table(forth.T)))
    forth, back = (
        np.stack([np.concatenate([high, low, high]) for high, low in (pair[way] for pair in fine)])
        for way in (0, 1)
    )
    return enter, leave, turn_cos, turn_sin, forth, back


def mxu(left, right):
    return jnp.dot(left, right, preferred_element_type=jnp.float32)


def halves(value):
    high = value.astype(jnp.bfloat16)
    low = (value - high.astype(jnp.float32)).astype(jnp.bfloat16)
    return high, low


class Stages:
    def __init__(self, cos_ref, sin_ref, enter_ref, leave_ref, forth_ref, back_ref):
        self.cos_ref = cos_ref
        self.sin_ref = sin_ref
        self.enter_ref = enter_ref
        self.leave_ref = leave_ref
        self.forth_ref = forth_ref
        self.back_ref = back_ref

    def put(self, pair, odd, rows, real, imag):
        for part, value in enumerate((real, imag)):
            lanes = slice(part * HALF, (part + 1) * HALF)
            for ref, piece in zip(pair, halves(value)):
                ref[odd, rows, lanes] = piece

    def both(self, pair, matrix_ref, odd, rows):
        high = pair[0][odd, rows, :]
        return mxu(jnp.concatenate([pair[1][odd, rows, :], high, high], axis=1), matrix_ref[odd])

    def turns(self, tile):
        return self.cos_ref[tile : tile + TILE, :], self.sin_ref[tile : tile + TILE, :]

    def enter(self, taken, pair, start):
        first = mxu(self.enter_ref[...], jnp.concatenate([taken, taken], axis=0))
        for tile in range(0, KEPT, TILE):
            real = first[2 * tile : 2 * tile + TILE]
            imag = first[2 * tile + TILE : 2 * tile + 2 * TILE]
            turn_cos, turn_sin = self.turns(tile)
            turned_real = real * turn_cos + imag * turn_sin
            turned_imag = imag * turn_cos - real * turn_sin
            rows = slice(start + tile, start + tile + TILE)
            near_real, far_real = turned_real[:, :HALF], turned_real[:, HALF:]
            near_imag, far_imag = turned_imag[:, :HALF], turned_imag[:, HALF:]
            self.put(pair, 0, rows, near_real + far_real, near_imag + far_imag)
            self.put(pair, 1, rows, near_real - far_real, near_imag - far_imag)

    def forth(self, pair, spec_ref, rows):
        for odd in (0, 1):
            spec_ref[odd, rows, :] = self.both(pair, self.forth_ref, odd, rows)

    def back(self, pair, turn_ref, rows):
        for odd in (0, 1):
            turn_ref[odd, rows, :] = self.both(pair, self.back_ref, odd, rows)

    def leave(self, turn_ref, start):
        pieces = [[], [], [], []]
        for tile in range(0, KEPT, TILE):
            rows = slice(start + tile, start + tile + TILE)
            turn_cos, turn_sin = self.turns(tile)
            even, odd = turn_ref[0, rows, :], turn_ref[1, rows, :]
            near, far = even + odd, even - odd
            real = jnp.concatenate([near[:, :HALF], far[:, :HALF]], axis=1)
            imag = jnp.concatenate([near[:, HALF:], far[:, HALF:]], axis=1)
            real_high, real_low = halves(real * turn_cos - imag * turn_sin)
            imag_high, imag_low = halves(imag * turn_cos + real * turn_sin)
            for kept, piece in zip(pieces, (real_high, imag_high, real_low, imag_low)):
                kept.append(piece)
        result = mxu(self.leave_ref[...], jnp.concatenate(sum(pieces, []), axis=0))
        return result[:BLOCKS] + result[BLOCKS:]


MEMBERS = SIGNALS // GROUPS_HERE
PAIRS = 2 * MEMBERS
GROUP_ROWS = PAIRS * KEPT


def every(row):
    return pl.ds(row, BLOCKS, stride=SIGNALS)


def spread(wide_ref, lane, received):
    wide_ref[lane] = received.astype(jnp.float32).reshape(BLOCKS * SIGNALS, HALF)


def gather(wide_ref, lane):
    return wide_ref[lane].reshape(BLOCKS, SIGNALS, HALF).astype(jnp.bfloat16)


def places(group, item):
    which, member = divmod(item, MEMBERS)
    row = member * GROUPS_HERE + group
    return ((2 * which, row), (2 * which + 1, row))


def spot(group, item, offset=0, size=KEPT):
    start = (group * PAIRS + item) * KEPT + offset
    return slice(start, start + size)


def lag_kernel(
    recv_ref,
    enter_ref,
    leave_ref,
    cos_ref,
    sin_ref,
    forth_ref,
    back_ref,
    lag_ref,
    spec_ref,
    wide_ref,
    high_ref,
    low_ref,
    high_lag_ref,
    low_lag_ref,
    turn_ref,
    wide_lag_ref,
):
    stages = Stages(cos_ref, sin_ref, enter_ref, leave_ref, forth_ref, back_ref)
    pair, joined = (high_ref, low_ref), (high_lag_ref, low_lag_ref)
    for lane in range(4):
        spread(wide_ref, lane, recv_ref[:, :, lane * HALF : (lane + 1) * HALF])
    def enter(group):
        for item in range(PAIRS):
            taken = jnp.concatenate(
                [wide_ref[lane, every(row), :] for lane, row in places(group, item)], axis=1
            ).astype(jnp.bfloat16)
            stages.enter(taken, pair, spot(group, item).start)

    enter(0)
    for group in range(GROUPS_HERE):
        if group + 1 < GROUPS_HERE:
            enter(group + 1)
        stages.forth(pair, spec_ref, slice(group * GROUP_ROWS, (group + 1) * GROUP_ROWS))
    for group in range(GROUPS_HERE):
        for odd in (0, 1):
            for tile in range(0, KEPT, TILE):
                real = imag = None
                for member in range(MEMBERS):
                    rows = spot(group, member, tile, TILE)
                    in_real, in_imag = spec_ref[odd, rows, :HALF], spec_ref[odd, rows, HALF:]
                    rows = spot(group, MEMBERS + member, tile, TILE)
                    cot_real, cot_imag = spec_ref[odd, rows, :HALF], spec_ref[odd, rows, HALF:]
                    more_real = cot_real * in_real + cot_imag * in_imag
                    more_imag = cot_imag * in_real - cot_real * in_imag
                    real = more_real if member == 0 else real + more_real
                    imag = more_imag if member == 0 else imag + more_imag
                start = group * KEPT + tile
                stages.put(joined, odd, slice(start, start + TILE), real, imag)
    for half in range(2):
        stages.back(joined, turn_ref, slice(half * 2 * KEPT, (half + 1) * 2 * KEPT))
    for group in range(GROUPS_HERE):
        result = stages.leave(turn_ref, group * KEPT)
        wide_lag_ref[0, every(group), :] = result[:, :HALF]
        wide_lag_ref[0, every(group + GROUPS_HERE), :] = result[:, HALF:]
    lag_ref[...] = gather(wide_lag_ref, 0)


def signal_kernel(
    skip_ref,
    recv_ref,
    spec_ref,
    wide_ref,
    enter_ref,
    leave_ref,
    cos_ref,
    sin_ref,
    forth_ref,
    back_ref,
    send_ref,
    wide_taps_ref,
    high_taps_ref,
    low_taps_ref,
    spec_taps_ref,
    high_ref,
    low_ref,
    turn_ref,
    wide_out_ref,
):
    stages = Stages(cos_ref, sin_ref, enter_ref, leave_ref, forth_ref, back_ref)
    taps_pair, pair = (high_taps_ref, low_taps_ref), (high_ref, low_ref)
    skip = jnp.concatenate([skip_ref[...], jnp.zeros((6, ROWS), jnp.float32)], axis=0)
    gains = pltpu.roll(skip, lax.rem(ROWS - position()[1] * GROUPS_HERE, ROWS), 1)
    spread(wide_taps_ref, 0, recv_ref[:, :, 4 * HALF :])
    for group in range(GROUPS_HERE):
        taken = jnp.concatenate(
            [
                wide_taps_ref[0, every(group), :],
                wide_taps_ref[0, every(group + GROUPS_HERE), :],
            ],
            axis=1,
        ).astype(jnp.bfloat16)
        stages.enter(taken, taps_pair, group * KEPT)
    size = GROUPS_HERE * KEPT // 2
    for part in range(2):
        stages.forth(taps_pair, spec_taps_ref, slice(part * size, (part + 1) * size))

    def multiply(group):
        for odd in (0, 1):
            for tile in range(0, KEPT, TILE):
                rows = slice(group * KEPT + tile, group * KEPT + tile + TILE)
                tap_real, tap_imag = spec_taps_ref[odd, rows, :HALF], spec_taps_ref[odd, rows, HALF:]
                for item in range(PAIRS):
                    rows = spot(group, item, tile, TILE)
                    real, imag = spec_ref[odd, rows, :HALF], spec_ref[odd, rows, HALF:]
                    turn = tap_imag if item < MEMBERS else -tap_imag
                    stages.put(
                        pair,
                        odd,
                        rows,
                        real * tap_real - imag * turn,
                        real * turn + imag * tap_real,
                    )

    def back(group):
        size = GROUP_ROWS // 2
        for part in range(2):
            start = group * GROUP_ROWS + part * size
            stages.back(pair, turn_ref, slice(start, start + size))

    def leave(group):
        for item in range(PAIRS):
            result = stages.leave(turn_ref, spot(group, item).start)
            member = item % MEMBERS
            gain = gains[member : member + 1, group : group + 1]
            for part, (lane, row) in enumerate(places(group, item)):
                direct = wide_ref[lane, every(row), :] * gain
                wide_out_ref[lane, every(row), :] = (
                    result[:, part * HALF : (part + 1) * HALF] + direct
                )

    for stage in (multiply, back, leave):
        for group in range(GROUPS_HERE):
            stage(group)
    for lane in range(4):
        send_ref[:, :, lane * HALF : (lane + 1) * HALF] = gather(wide_out_ref, lane)


def spectral(received, skip_gain, send_lag):
    constants = [jnp.asarray(table) for table in tables()]
    signal_rows, group_rows = GROUPS_HERE * GROUP_ROWS, GROUPS_HERE * KEPT
    whole = pl.BlockSpec(memory_space=pltpu.VMEM)
    params = pltpu.CompilerParams(vmem_limit_bytes=24 * 1024 * 1024)
    lag, spec, wide = pl.pallas_call(
        lag_kernel,
        out_shape=(
            jax.ShapeDtypeStruct((BLOCKS, SIGNALS, HALF), jnp.bfloat16),
            jax.ShapeDtypeStruct((2, signal_rows, ROWS), jnp.float32),
            jax.ShapeDtypeStruct((4, BLOCKS * SIGNALS, HALF), jnp.float32),
        ),
        in_specs=[whole] * 7,
        out_specs=(whole,) * 3,
        scratch_shapes=[
            pltpu.VMEM((2, signal_rows, ROWS), jnp.bfloat16),
            pltpu.VMEM((2, signal_rows, ROWS), jnp.bfloat16),
            pltpu.VMEM((2, group_rows, ROWS), jnp.bfloat16),
            pltpu.VMEM((2, group_rows, ROWS), jnp.bfloat16),
            pltpu.VMEM((2, group_rows, ROWS), jnp.float32),
            pltpu.VMEM((1, BLOCKS * SIGNALS, HALF), jnp.float32),
        ],
        compiler_params=params,
        cost_estimate=pl.CostEstimate(
            flops=3_000_000_000, bytes_accessed=5_000_000, transcendentals=0
        ),
        name="lags",
    )(received, *constants)
    moved = send_lag(lag)
    signals = pl.pallas_call(
        signal_kernel,
        out_shape=jax.ShapeDtypeStruct((BLOCKS, SIGNALS, 4 * HALF), jnp.bfloat16),
        in_specs=[whole] * 10,
        out_specs=whole,
        scratch_shapes=[
            pltpu.VMEM((1, BLOCKS * SIGNALS, HALF), jnp.float32),
            pltpu.VMEM((2, group_rows, ROWS), jnp.bfloat16),
            pltpu.VMEM((2, group_rows, ROWS), jnp.bfloat16),
            pltpu.VMEM((2, group_rows, ROWS), jnp.float32),
            pltpu.VMEM((2, signal_rows, ROWS), jnp.bfloat16),
            pltpu.VMEM((2, signal_rows, ROWS), jnp.bfloat16),
            pltpu.VMEM((2, signal_rows, ROWS), jnp.float32),
            pltpu.VMEM((4, BLOCKS * SIGNALS, HALF), jnp.float32),
        ],
        compiler_params=params,
        cost_estimate=pl.CostEstimate(
            flops=3_000_000_000, bytes_accessed=5_000_000, transcendentals=0
        ),
        name="signals",
    )(skip_gain, received, spec, wide, *constants)
    return jnp.concatenate([signals, moved], axis=2)


RING = 8


def shift(row, column):
    return (row + RING // 2 * (column % 2)) % RING


def position():
    seat, plane = lax.axis_index("seq"), lax.axis_index("chan")
    row, column = lax.div(seat, RING), lax.rem(seat, RING)
    held = lax.rem(RING - plane + row + RING // 2 * lax.rem(column, 2), RING) * RING + column
    return plane, held


def holders(plane):
    return [
        [lax.rem(first - RING // 2 * odd + RING + plane, RING) for odd in (0, 1)]
        for first in range(RING)
    ]


def gate_kernel(
    out_gate_ref,
    in_gate_ref,
    values_ref,
    taps_ref,
    cot_ref,
    send_ref,
    gates_ref,
    held_taps_ref,
    arrived,
):
    sources = (in_gate_ref, values_ref, cot_ref, out_gate_ref)
    copies = [
        pltpu.make_async_copy(source, gates_ref.at[slot], arrived.at[slot])
        for slot, source in enumerate(sources)
    ]
    copies.append(pltpu.make_async_copy(taps_ref, held_taps_ref, arrived.at[len(sources)]))
    for copy in copies:
        copy.start()

    row = lax.broadcasted_iota(jnp.int32, (2 * ROWS, 2 * ROWS), 0)
    column = lax.broadcasted_iota(jnp.int32, (2 * ROWS, 2 * ROWS), 1)
    parted = (row == column % ROWS * 2 + column // ROWS).astype(jnp.float32)
    parted = parted.astype(jnp.bfloat16)
    plain = (row == column)[:ROWS, :ROWS].astype(jnp.float32).astype(jnp.bfloat16)

    def turned(value, order):
        return lax.dot_general(
            value, order, (((0,), (0,)), ((), ())), preferred_element_type=jnp.float32
        ).astype(jnp.bfloat16)

    owners = holders(position()[0])

    def send(part, lanes, value):
        rows = slice(part * GROUPS_HERE, (part + 1) * GROUPS_HERE)
        value = value.reshape(BLOCKS, GROUPS_HERE, -1)
        for first in range(RING):
            for second in range(RING):
                send_ref[owners[first][second % 2], second, rows, lanes] = value[
                    first * RING + second
                ]

    for which in range(2):
        left, right = 2 * which, 2 * which + 1
        copies[left].wait()
        copies[right].wait()
        product = gates_ref[left].reshape(2 * ROWS, ROWS).astype(jnp.float32) * gates_ref[
            right
        ].reshape(2 * ROWS, ROWS).astype(jnp.float32)
        signal = turned(product.astype(jnp.bfloat16), parted)
        for member in range(2):
            send(
                member,
                slice(which * ROWS, (which + 1) * ROWS),
                signal[:, member * ROWS : (member + 1) * ROWS],
            )
    copies[-1].wait()
    taps = turned(held_taps_ref[...], plain)
    for half in range(2):
        send(half, slice(2 * ROWS, None), taps[:, half * HALF : (half + 1) * HALF])


def gated_chunks(out_gate, in_gate, values_in, filter_taps, out_cotangent):
    return pl.pallas_call(
        gate_kernel,
        out_shape=jax.ShapeDtypeStruct((RING, RING, SIGNALS, 5 * HALF), jnp.bfloat16),
        in_specs=[pl.BlockSpec(memory_space=pltpu.HBM)] * 5,
        out_specs=pl.BlockSpec(memory_space=pltpu.VMEM),
        scratch_shapes=[
            pltpu.VMEM((4, ROWS, 2, ROWS), jnp.bfloat16),
            pltpu.VMEM((ROWS, ROWS), jnp.bfloat16),
            pltpu.SemaphoreType.DMA((5,)),
        ],
        compiler_params=pltpu.CompilerParams(vmem_limit_bytes=16 * 1024 * 1024),
        cost_estimate=pl.CostEstimate(
            flops=400_000_000, bytes_accessed=2_000_000, transcendentals=0
        ),
        name="gates",
    )(
        *(
            pltpu.with_memory_space_constraint(value, pltpu.HBM)
            for value in (out_gate, in_gate, values_in, filter_taps, out_cotangent)
        )
    )


def outcome_kernel(
    scale,
    returned_ref,
    out_gate_ref,
    in_gate_ref,
    values_ref,
    cot_ref,
    mixed_ref,
    grad_out_gate_ref,
    grad_in_gate_ref,
    grad_values_ref,
    grad_filter_ref,
    ordered_ref,
    results_ref,
    sums_ref,
    left,
):
    owners = holders(position()[0])
    for first in range(RING):
        for second in range(RING):
            ordered_ref[first * RING + second] = returned_ref[
                owners[first][second % 2], second, :, : 2 * ROWS
            ]
    row = lax.broadcasted_iota(jnp.int32, (2 * ROWS, 2 * ROWS), 0)
    column = lax.broadcasted_iota(jnp.int32, (2 * ROWS, 2 * ROWS), 1)
    parted = (column == row % 2 * ROWS + row // 2).astype(jnp.float32).astype(jnp.bfloat16)
    copies = []
    results = (
        (mixed_ref, out_gate_ref),
        (grad_out_gate_ref, cot_ref),
        (grad_in_gate_ref, values_ref),
        (grad_values_ref, in_gate_ref),
    )
    for which in range(2):
        lanes = slice(which * ROWS, (which + 1) * ROWS)
        turned = jnp.concatenate(
            [
                ordered_ref[:, part * GROUPS_HERE : (part + 1) * GROUPS_HERE, lanes].reshape(
                    ROWS, ROWS
                )
                for part in range(2)
            ],
            axis=1,
        )
        signal = lax.dot_general(
            parted, turned, (((1,), (1,)), ((), ())), preferred_element_type=jnp.float32
        )
        for slot in (2 * which, 2 * which + 1):
            result_ref, gate_ref = results[slot]
            gate = gate_ref[...].reshape(2 * ROWS, ROWS).astype(jnp.float32)
            results_ref[slot] = (signal * gate).astype(jnp.bfloat16).reshape(ROWS, 2, ROWS)
            copies.append(
                pltpu.make_async_copy(results_ref.at[slot], result_ref, left.at[slot])
            )
            copies[-1].start()
    for second in range(RING):
        total = returned_ref[0, second, :, 2 * ROWS :].astype(jnp.float32)
        for first in range(1, RING):
            total += returned_ref[first, second, :, 2 * ROWS :].astype(jnp.float32)
        total = total * scale
        rows = slice(second * GROUPS_HERE, (second + 1) * GROUPS_HERE)
        sums_ref[rows, :HALF] = total[:GROUPS_HERE]
        sums_ref[rows, HALF:] = total[GROUPS_HERE:]
    copies.append(pltpu.make_async_copy(sums_ref, grad_filter_ref, left.at[len(results)]))
    copies[-1].start()
    for copy in copies:
        copy.wait()


def outcomes(scale, returned, out_gate, in_gate, values_in, out_cotangent):
    whole = pl.BlockSpec(memory_space=pltpu.VMEM)
    signal = jax.ShapeDtypeStruct((ROWS, 2, ROWS), jnp.bfloat16)
    return pl.pallas_call(
        functools.partial(outcome_kernel, scale),
        out_shape=(signal,) * 4
        + (jax.ShapeDtypeStruct((RING * GROUPS_HERE, ROWS), jnp.float32),),
        in_specs=[whole] * 5,
        out_specs=(pl.BlockSpec(memory_space=pl.ANY),) * 5,
        scratch_shapes=[
            pltpu.VMEM((BLOCKS, SIGNALS, 2 * ROWS), jnp.bfloat16),
            pltpu.VMEM((4, ROWS, 2, ROWS), jnp.bfloat16),
            pltpu.VMEM((RING * GROUPS_HERE, ROWS), jnp.float32),
            pltpu.SemaphoreType.DMA((5,)),
        ],
        compiler_params=pltpu.CompilerParams(vmem_limit_bytes=16 * 1024 * 1024),
        cost_estimate=pl.CostEstimate(
            flops=400_000_000, bytes_accessed=3_000_000, transcendentals=0
        ),
        name="outcomes",
    )(returned, out_gate, in_gate, values_in, out_cotangent)


def exchange(value, axis):
    return lax.all_to_all(value, axis, split_axis=0, concat_axis=0, tiled=True)


def local(out_gate, in_gate, values_in, filter_taps, skip_gain, out_cotangent):
    row_count, member_count, group_count = out_gate.shape
    chan_count = lax.axis_size("chan")

    def send_lag(lag):
        pairs = [
            (
                (first * RING + second) * RING + level,
                (first * RING + second) * RING + (shift(first, second) - level) % RING,
            )
            for first in range(RING)
            for second in range(RING)
            for level in range(RING)
        ]
        return lax.ppermute(lag, ("seq", "chan"), pairs)

    outgoing = gated_chunks(out_gate, in_gate, values_in, filter_taps, out_cotangent)
    received = exchange(outgoing.reshape(BLOCKS, SIGNALS, 5 * HALF), "seq")
    returned = exchange(spectral(received, skip_gain, send_lag), "seq")
    norm_factor = 1.0 / math.sqrt(BLOCKS * row_count * member_count * chan_count)
    *gradients, filter_sum = outcomes(
        norm_factor,
        returned.reshape(RING, RING, SIGNALS, 5 * HALF),
        out_gate,
        in_gate,
        values_in,
        out_cotangent,
    )
    return (*gradients, filter_sum.T)


def solution(mesh):
    in_specs = (
        P("seq", "chan", None),
        P("seq", "chan", None),
        P("seq", "chan", None),
        P("seq", None),
        P("chan", None),
        P("seq", "chan", None),
    )
    out_specs = (
        P("seq", "chan", None),
        P("seq", "chan", None),
        P("seq", "chan", None),
        P("seq", "chan", None),
        P("seq", "chan"),
    )
    return jax.shard_map(local, mesh=mesh, in_specs=in_specs, out_specs=out_specs, check_vma=False)
```
